256 devices in a mesh: section: 16 (over z, x_lo), dp: 16 (over y, x_hi, core).
Axes of the slice: x: 4 (x_hi: 2, x_lo: 2; x = x_hi * 2 + x_lo), y: 4, z: 8, core: 2. Of those that a mesh axis runs over, the one named last changes fastest.
Arguments:
- coeffs: bfloat16 [2, 2048, 256], P(None, 'dp'), may hold values from -6 to 6
- cotangent: bfloat16 [2, 2048, 256], P(None, 'dp'), may hold values from -0.1875 to 0.1875
- segment_ids: int32 [2, 2048], P(None, 'dp'), may hold values from 0 to 127, never falling along the last dimension, each value on 1 to 32 neighbouring positions
- basis_matrix: bfloat16 [4096, 256], replicated, may hold values from -0.375 to 0.375
- section_gains: float32 [16, 4096], P('section'), may hold values from 0.5 to 1.5
- value_weight: bfloat16 [16, 4096, 1024], P('section'), may hold values from -0.09375 to 0.09375
- out_weight: bfloat16 [16, 1024, 256], P('section'), may hold values from -0.1875 to 0.1875
Outputs:
- grad_value: float32 [16, 4096, 1024], P('section', 'dp')
- grad_out: float32 [16, 1024, 256], P('section', 'dp')
- grad_gain: float32 [16, 4096], P('section', 'dp')
The draws below stay inside these ranges and needn't reach their ends.
All inputs are finite; a program needn't handle non-finite values.
Results may differ from the reference program's by a relative error of at most 0.034.
Values may be sent and summed in bfloat16 or wider, within the bound.
A program may use at most 128 MiB of HBM per device.

```python
import math
import jax
import jax.numpy as jnp
import numpy as np
from jax import lax

D = 4096
KV = 1024
K = 256
ROWS = 128
MICRO = 2
SECTIONS = 16
TOKENS_MB = 2048


def level_of(key, dims, cuts, least, top_value):
    gain = 1.0
    for axis_at, blocks in cuts:
        draws = jax.random.uniform(jax.random.fold_in(jax.random.fold_in(key, 6), axis_at), (blocks,), jnp.float32, least / len(cuts), top_value / len(cuts))
        gain = gain * jnp.repeat(jnp.exp(draws), dims[axis_at] // blocks).reshape((-1,) + (1,) * (len(dims) - 1 - axis_at))
    return gain


def profile(number_of, total, reach, lean):
    portions = [(1 << 20) // math.isqrt(standing ** lean) + 1 for standing in range(2, number_of + 1)]
    surplus, given = total - reach - (number_of - 1), [1] * (number_of - 1)
    while surplus > 0:
        free = [i for i in range(number_of - 1) if given[i] < reach]
        pool, left = sum([portions[i] for i in free]), surplus
        for i in free:
            addition = min(reach - given[i], max(1, left * portions[i] // pool), surplus)
            given[i] = given[i] + addition
            surplus = surplus - addition
    return np.array([reach] + given)


def ragged(own_key, amount, total, most, lean):
    if amount == 2:
        one = jax.random.randint(own_key, (), max(1, total - most), min(most, total - 1) + 1)
        return jnp.stack([one, total - one])
    sizes = jnp.asarray(profile(amount, total, most, lean), jnp.int32)
    twos = (amount - 1) // 2
    source_of, receiver = sizes[1:1 + 2 * twos:2], sizes[2:2 + 2 * twos:2]
    slack = jnp.minimum(source_of - 1, most - receiver)
    moved = jax.random.randint(jax.random.fold_in(own_key, 1), (twos,), 0, 1 << 20) % (slack + 1)
    sizes = sizes.at[1:1 + 2 * twos:2].set(source_of - moved).at[2:2 + 2 * twos:2].set(receiver + moved)
    return sizes[jax.random.permutation(jax.random.fold_in(own_key, 2), amount)]


def scatter_about(key, shape, width, most, split=(), held_as=jnp.bfloat16):
    level = level_of(key, shape, split, -0.22, 0.18) if split else 1.0
    array = jax.random.normal(key, shape, jnp.float32) * width * level
    return jnp.minimum(jnp.maximum(array, -most), most).astype(held_as)


def setup_inputs(seed: int = 0) -> dict:
    streams_of = jax.random.split(jax.random.key(seed), 8)
    return {
        "coeffs": scatter_about(streams_of[0], (MICRO, TOKENS_MB, K), 1.0, 6.0, ((1, 16),)),
        "cotangent": scatter_about(streams_of[1], (MICRO, TOKENS_MB, K), 0.03, 0.1875, ((1, 16),)),
        "segment_ids": jax.vmap(lambda own: jnp.searchsorted(jnp.cumsum(ragged(own, TOKENS_MB // 16, TOKENS_MB, 32, 2)), jnp.arange(TOKENS_MB), side="right"))(jax.random.split(streams_of[2], MICRO)).reshape((MICRO, TOKENS_MB)).astype(jnp.int32),
        "basis_matrix": scatter_about(streams_of[3], (D, K), K ** -0.5, 0.375),
        "section_gains": jnp.clip(1.0 + 0.1 * jax.random.normal(streams_of[4], (SECTIONS, D), jnp.float32), 0.5, 1.5),
        "value_weight": scatter_about(streams_of[5], (SECTIONS, D, KV), D ** -0.5, 0.09375, ((0, 16),)),
        "out_weight": scatter_about(streams_of[6], (SECTIONS, KV, K), KV ** -0.5, 0.1875, ((0, 16),)),
    }


EPS = 1e-05

def mixing_blocks(segment_ids):
    blocks = segment_ids.reshape(-1, ROWS)
    positions = jnp.arange(ROWS)
    same_segment = (blocks[:, :, None] == blocks[:, None, :]) & (positions[None, :, None] >= positions[None, None, :])
    weights = same_segment.astype(jnp.float32)
    return (weights / lax.optimization_barrier(jnp.sum(weights, axis=2, keepdims=True))).astype(jnp.bfloat16)

def normalize(section_coeff, basis_matrix):
    rebuilt = jnp.dot(section_coeff, basis_matrix.T, preferred_element_type=jnp.float32)
    inv_rms = lax.rsqrt(lax.optimization_barrier(jnp.mean(rebuilt * rebuilt, axis=1, keepdims=True)) + EPS)
    return (rebuilt, inv_rms)

def pool_rows(mixing, values):
    blocks = values.reshape(mixing.shape[0], ROWS, -1).astype(jnp.float32)
    pooled = jnp.einsum('bij,bjk->bik', mixing.astype(jnp.float32), blocks)
    return pooled.reshape(values.shape).astype(jnp.bfloat16)

def pool_back(mixing, grads):
    blocks = grads.reshape(mixing.shape[0], ROWS, -1).astype(jnp.float32)
    pooled = jnp.einsum('bji,bjk->bik', mixing.astype(jnp.float32), blocks)
    return pooled.reshape(grads.shape).astype(jnp.bfloat16)

def section_values(section_coeff, basis_matrix, mixing, section_gain, section_value):
    rebuilt, inv_rms = normalize(section_coeff, basis_matrix)
    normed = (rebuilt * inv_rms * section_gain).astype(jnp.bfloat16)
    values = jnp.dot(normed, section_value, preferred_element_type=jnp.float32).astype(jnp.bfloat16)
    return (rebuilt, inv_rms, pool_rows(mixing, values))

def reference(coeffs, cotangent, segment_ids, basis_matrix, section_gains, value_weight, out_weight):
    mixing = mixing_blocks(segment_ids)
    flat_coeffs = coeffs.reshape(-1, coeffs.shape[2])

    def forward(section_coeff, params):
        section_gain, section_value, section_out = params
        rebuilt, inv_rms, pooled = section_values(section_coeff, basis_matrix, mixing, section_gain, section_value)
        update = jnp.dot(pooled, section_out, preferred_element_type=jnp.float32)
        return ((section_coeff.astype(jnp.float32) + update).astype(jnp.bfloat16), section_coeff)
    final_coeffs, inputs = lax.scan(forward, flat_coeffs, (section_gains, value_weight, out_weight))

    def backward(grad_next, params):
        section_coeff, section_gain, section_value, section_out = params
        rebuilt, inv_rms, pooled = section_values(section_coeff, basis_matrix, mixing, section_gain, section_value)
        grad_out = jnp.dot(pooled.T, grad_next, preferred_element_type=jnp.float32)
        back_pooled = jnp.dot(grad_next, section_out.T, preferred_element_type=jnp.float32).astype(jnp.bfloat16)
        back_values = pool_back(mixing, back_pooled)
        scaled_coeff = (section_coeff.astype(jnp.float32) * inv_rms).astype(jnp.bfloat16)
        factor = jnp.dot(scaled_coeff.T, back_values, preferred_element_type=jnp.float32)
        grad_value = jnp.dot(section_gain[:, None] * basis_matrix.astype(jnp.float32), factor, precision=lax.Precision.HIGHEST)
        back_normed = jnp.dot(back_values, section_value.T, preferred_element_type=jnp.float32)
        unit_rows = rebuilt * inv_rms
        grad_gain = lax.optimization_barrier(jnp.sum(back_normed * unit_rows, axis=0))
        back_unit = back_normed * section_gain
        back_rebuilt = (inv_rms * (back_unit - unit_rows * lax.optimization_barrier(jnp.mean(back_unit * unit_rows, axis=1, keepdims=True)))).astype(jnp.bfloat16)
        grad_now = (grad_next.astype(jnp.float32) + jnp.dot(back_rebuilt, basis_matrix, preferred_element_type=jnp.float32)).astype(jnp.bfloat16)
        return (grad_now, (grad_value, grad_out, grad_gain))
    first_grad, results = lax.scan(backward, cotangent.reshape(-1, cotangent.shape[2]), (inputs, section_gains, value_weight, out_weight), reverse=True)
    return (results[0], results[1], results[2])
```

```python
import functools

import jax
import jax.numpy as jnp
from jax import lax
from jax.experimental import pallas as pl
from jax.experimental.pallas import tpu as pltpu
from jax.sharding import PartitionSpec as P

EPS = 1e-05
F32 = jnp.float32
BF16 = jnp.bfloat16


def mm(a, b, dims=((1,), (0,))):
    return lax.dot_general(a, b, (dims, ((), ())), preferred_element_type=F32)


def mixing_pair(seg_row):
    rows = seg_row.shape[1]
    across = jnp.broadcast_to(seg_row, (rows, rows))
    down = across.T
    i = lax.broadcasted_iota(jnp.int32, (rows, rows), 0)
    j = lax.broadcasted_iota(jnp.int32, (rows, rows), 1)
    same = across == down
    low = jnp.where(same & (j <= i), 1.0, 0.0).astype(F32)
    high = jnp.where(same & (i <= j), 1.0, 0.0).astype(F32)
    mixing = (low / jnp.sum(low, axis=1, keepdims=True)).astype(BF16)
    mixing_t = (high / jnp.sum(high, axis=0, keepdims=True)).astype(BF16)
    return mixing, mixing_t


def chain(width, n_ref, gram_ref, c_ref, cot_ref, seg_ref, f_ref, xs, ps, es, hs, invs):
    sections = n_ref.shape[0]
    micros = c_ref.shape[0]
    gram = gram_ref[...]
    gram_b = gram.astype(BF16)
    mixings = [mixing_pair(seg_ref[m : m + 1, :].astype(F32)) for m in range(micros)]
    cs = [c_ref[m].astype(F32) for m in range(micros)]
    hh = [mm(c_ref[m], gram_b) for m in range(micros)]
    for s in range(sections):
        n = n_ref[s]
        ng = mm(n, gram_b).astype(BF16)
        for m in range(micros):
            cb = cs[m].astype(BF16)
            ms = jnp.sum(cs[m] * hh[m], axis=1, keepdims=True) * (1.0 / width)
            inv = lax.rsqrt(jnp.maximum(ms, 0.0) + EPS)
            e = mm(cb, n)
            f = mm(cb, ng)
            xs[s, m] = (inv * cs[m]).astype(BF16)
            es[s, m] = e
            hs[s, m] = hh[m]
            invs[s, m] = jnp.broadcast_to(inv, invs.shape[2:])
            y = mm(mixings[m][0], (inv * e).astype(BF16))
            z = mm(mixings[m][0], (inv * f).astype(BF16))
            cs[m] = cs[m] + y
            hh[m] = hh[m] + z
    gs = [cot_ref[m].astype(F32) for m in range(micros)]
    for s in reversed(range(sections)):
        n = n_ref[s]
        for m in range(micros):
            p = mm(mixings[m][1], gs[m].astype(BF16))
            pb = p.astype(BF16)
            ps[s, m] = pb
            q = mm(pb, n, ((1,), (1,)))
            inv = invs[s, m][:, :1]
            t = jnp.sum(p * es[s, m], axis=1, keepdims=True)
            gs[m] = gs[m] + inv * q - (inv * inv * inv * t * (1.0 / width)) * hs[s, m]
    own = lax.axis_index("section")
    total = mm(xs[own, 0], ps[own, 0], ((0,), (0,)))
    for m in range(1, micros):
        total = total + mm(xs[own, m], ps[own, m], ((0,), (0,)))
    f_ref[...] = total


def run_chain(n_all, gram, coeffs, cotangent, segments, width):
    sections, sub, _ = n_all.shape
    micros, rows, _ = coeffs.shape
    whole = pl.BlockSpec(memory_space=pltpu.VMEM)
    return pl.pallas_call(
        functools.partial(chain, width),
        out_shape=jax.ShapeDtypeStruct((sub, sub), F32),
        in_specs=[whole] * 5,
        out_specs=whole,
        scratch_shapes=[
            pltpu.VMEM((sections, micros, rows, sub), BF16),
            pltpu.VMEM((sections, micros, rows, sub), BF16),
            pltpu.VMEM((sections, micros, rows, sub), F32),
            pltpu.VMEM((sections, micros, rows, sub), F32),
            pltpu.VMEM((sections, micros, rows, 128), F32),
        ],
        compiler_params=pltpu.CompilerParams(vmem_limit_bytes=48 * 1024 * 1024),
    )(n_all, gram, coeffs, cotangent, segments)


def shards(coeffs, cotangent, segment_ids, basis_matrix, section_gains, value_weight, out_weight):
    replicas = lax.axis_size("dp")
    replica = lax.axis_index("dp")
    gain = section_gains[0]
    value = value_weight[0]
    out = out_weight[0]
    width, inner = value.shape
    rows = width // replicas
    cols = inner // replicas
    scaled_basis = (gain[:, None] * basis_matrix.astype(F32)).astype(BF16)
    folded = mm(scaled_basis, value, ((0,), (0,))).astype(BF16)
    step = mm(folded, out).astype(BF16)
    steps = lax.all_gather(step, "section")
    gram = mm(basis_matrix, basis_matrix, ((0,), (0,)))
    factor_part = run_chain(steps, gram, coeffs, cotangent, segment_ids, width)
    factor = lax.psum(factor_part.astype(BF16), "dp")
    wide = mm(factor, out, ((1,), (1,))).astype(BF16)
    own_basis = lax.dynamic_slice_in_dim(basis_matrix, replica * rows, rows, 0)
    own_gain = lax.dynamic_slice_in_dim(gain, replica * rows, rows, 0)
    own_value = lax.dynamic_slice_in_dim(value, replica * rows, rows, 0)
    plain = mm(own_basis, wide)
    grad_value = own_gain[:, None] * plain
    grad_gain = jnp.sum(plain * own_value.astype(F32), axis=1)
    own_folded = lax.dynamic_slice_in_dim(folded, replica * cols, cols, 1)
    grad_out = mm(own_folded, factor, ((0,), (0,)))
    return (grad_value[None], grad_out[None], grad_gain[None])


def solution(mesh):
    placed = (
        P(None, "dp", None),
        P(None, "dp", None),
        P(None, "dp"),
        P(),
        P("section", None),
        P("section", None, None),
        P("section", None, None),
    )
    return jax.shard_map(
        shards,
        mesh=mesh,
        in_specs=placed,
        out_specs=(P("section", "dp", None), P("section", "dp", None), P("section", "dp")),
        check_vma=False,
    )
```

```python
import functools

import jax
import jax.numpy as jnp
from jax import lax
from jax.experimental import pallas as pl
from jax.experimental.pallas import tpu as pltpu
from jax.sharding import PartitionSpec as P

EPS = 1e-05
MESH = pl.DeviceIdType.MESH
F32 = jnp.float32
BF16 = jnp.bfloat16


def mm(a, b, dims=((1,), (0,))):
    return lax.dot_general(a, b, (dims, ((), ())), preferred_element_type=F32)


def mixing_pair(seg_row):
    rows = seg_row.shape[1]
    across = jnp.broadcast_to(seg_row, (rows, rows))
    down = across.T
    i = lax.broadcasted_iota(jnp.int32, (rows, rows), 0)
    j = lax.broadcasted_iota(jnp.int32, (rows, rows), 1)
    same = across == down
    low = jnp.where(same & (j <= i), 1.0, 0.0).astype(F32)
    high = jnp.where(same & (i <= j), 1.0, 0.0).astype(F32)
    mixing = (low / jnp.sum(low, axis=1, keepdims=True)).astype(BF16)
    mixing_t = (high / jnp.sum(high, axis=0, keepdims=True)).astype(BF16)
    return mixing, mixing_t


class Place:
    def __init__(self):
        self.s = lax.axis_index("section")
        self.d = lax.axis_index("dp")
        self.z = self.s // 2
        self.xl = self.s % 2
        self.y = self.d // 4
        self.xh = (self.d // 2) % 2
        self.core = self.d % 2
        self.x = self.xh * 2 + self.xl

    def dp_peer(self, k):
        return (self.s, (self.d + k) % 16)

    def z_peer(self, k):
        return (((self.z + k) % 8) * 2 + self.xl, self.d)

    def y_peer(self, k):
        return (self.s, ((self.y + k) % 4) * 4 + self.xh * 2 + self.core)

    def x_peer(self, k):
        x = (self.x + k) % 4
        return (self.z * 2 + x % 2, self.y * 4 + (x // 2) * 2 + self.core)

    def core_peer(self):
        return (self.s, self.y * 4 + self.xh * 2 + (self.core + 1) % 2)


def piece_of(d):
    return (d % 2) * 8 + d // 2


def greet(peers):
    barrier = pltpu.get_barrier_semaphore()
    for peer in peers:
        pl.semaphore_signal(barrier, inc=1, device_id=peer, device_id_type=MESH)
    pl.semaphore_wait(barrier, len(peers))


def send(src, dst, send_sem, recv_sem, peer):
    copy = pltpu.make_async_remote_copy(
        src_ref=src, dst_ref=dst, send_sem=send_sem, recv_sem=recv_sem,
        device_id=peer, device_id_type=MESH,
    )
    copy.start()
    return copy


def reduce_pieces(at, part, part_b, slots, send_sem, recv_sem):
    part_b[...] = part[...].astype(BF16)
    copies = []
    for k in range(1, 16):
        copies.append(
            send(part_b.at[piece_of((at.d + k) % 16)], slots.at[k], send_sem.at[k], recv_sem.at[k], at.dp_peer(k))
        )
    total = part[piece_of(at.d)]
    for k in range(1, 16):
        copies[k - 1].wait_recv()
        total = total + slots[k].astype(F32)
    for copy in copies:
        copy.wait_send()
    return total


def fold_and_gather(
    basis_hbm, gain_ref, value_hbm, out_hbm, all_ref, gram_ref, folded_ref,
    basis, basis_own, value_own, value_cols, out, gain_pad, part, part_b, slots,
    load_sem, rs_send, rs_recv, z_send, z_recv, h0_send, h0_recv, h1_send, h1_recv, c_send, c_recv,
):
    at = Place()
    rows = pl.ds(pl.multiple_of(at.d * 256, 256), 256)
    cols = pl.ds(pl.multiple_of((at.d // 2) * 128, 128), 128)
    loads = [
        pltpu.make_async_copy(value_hbm.at[0, rows, :], value_own, load_sem.at[0]),
        pltpu.make_async_copy(out_hbm.at[0], out, load_sem.at[1]),
        pltpu.make_async_copy(basis_hbm.at[rows, :], basis_own, load_sem.at[2]),
        pltpu.make_async_copy(basis_hbm, basis, load_sem.at[3]),
        pltpu.make_async_copy(value_hbm.at[0, :, cols], value_cols, load_sem.at[4]),
    ]
    for load in loads:
        load.start()
    peers = [at.dp_peer(k) for k in range(1, 16)] + [at.z_peer(k) for k in range(1, 8)]
    peers += [at.x_peer(1), at.x_peer(3)]
    greet(peers)
    gain_pad[...] = jnp.zeros_like(gain_pad)
    gain_pad[0:16, :] = gain_ref[...]
    gain_cols = gain_pad[...].T
    lane = lax.broadcasted_iota(jnp.int32, gain_cols.shape, 1)
    own_gain = jnp.sum(jnp.where(lane == at.d, gain_cols, 0.0), axis=1, keepdims=True)
    loads[0].wait()
    loads[1].wait()
    through = mm(value_own[...], out[...]).astype(BF16)
    loads[2].wait()
    scaled = (basis_own[...].astype(F32) * own_gain).astype(BF16)
    part[...] = mm(scaled, through, ((0,), (0,))).reshape(16, 16, 256)
    piece = reduce_pieces(at, part, part_b, slots, rs_send, rs_recv)

    own = all_ref.at[at.core, at.z % 2, at.y, at.xh, at.xl, at.z // 2]
    own[...] = piece.astype(BF16)
    over_z = [send(own, own, z_send.at[k], z_recv.at[k], at.z_peer(k)) for k in range(1, 8)]

    loads[3].wait()
    loads[4].wait()
    gram = jnp.zeros((256, 256), F32)
    folded = jnp.zeros((256, 128), F32)
    for i in range(16):
        chunk = basis[i * 256 : (i + 1) * 256, :]
        gram = gram + mm(chunk, chunk, ((0,), (0,)))
        scaled = (chunk.astype(F32) * gain_cols[:, i : i + 1]).astype(BF16)
        folded = folded + mm(scaled, value_cols[i * 256 : (i + 1) * 256, :], ((0,), (0,)))
    gram_ref[...] = gram
    folded_ref[...] = folded.astype(BF16)

    for copy in over_z:
        copy.wait_recv()
    own0 = all_ref.at[at.core, 0, at.y, at.xh, at.xl]
    own1 = all_ref.at[at.core, 1, at.y, at.xh, at.xl]
    x0 = [send(own0, own0, h0_send.at[k], h0_recv.at[k], at.x_peer(k)) for k in range(1, 4)]
    y1 = [send(own1, own1, h1_send.at[k], h1_recv.at[k], at.y_peer(k)) for k in range(1, 4)]
    for copy in x0:
        copy.wait_recv()
    row0 = all_ref.at[at.core, 0, at.y]
    y0 = [send(row0, row0, h0_send.at[3 + k], h0_recv.at[3 + k], at.y_peer(k)) for k in range(1, 4)]
    for copy in y1:
        copy.wait_recv()
    row1 = all_ref.at[at.core, 1, :, at.xh, at.xl]
    x1 = [send(row1, row1, h1_send.at[3 + k], h1_recv.at[3 + k], at.x_peer(k)) for k in range(1, 4)]
    for copy in y0 + x1:
        copy.wait_recv()
    half = all_ref.at[at.core]
    across = send(half, half, c_send, c_recv, at.core_peer())
    across.wait_recv()
    for copy in over_z + x0 + y1 + y0 + x1 + [across]:
        copy.wait_send()


def run_fold(basis, gain, value, out):
    vmem = pl.BlockSpec(memory_space=pltpu.VMEM)
    anywhere = pl.BlockSpec(memory_space=pl.ANY)
    dma = pltpu.SemaphoreType.DMA
    return pl.pallas_call(
        fold_and_gather,
        out_shape=(
            jax.ShapeDtypeStruct((2, 2, 4, 2, 2, 4, 16, 256), BF16),
            jax.ShapeDtypeStruct((256, 256), F32),
            jax.ShapeDtypeStruct((256, 128), BF16),
        ),
        in_specs=[anywhere, vmem, anywhere, anywhere],
        out_specs=(vmem, vmem, vmem),
        scratch_shapes=[
            pltpu.VMEM((4096, 256), BF16),
            pltpu.VMEM((256, 256), BF16),
            pltpu.VMEM((256, 1024), BF16),
            pltpu.VMEM((4096, 128), BF16),
            pltpu.VMEM((1024, 256), BF16),
            pltpu.VMEM((128, 256), F32),
            pltpu.VMEM((16, 16, 256), F32),
            pltpu.VMEM((16, 16, 256), BF16),
            pltpu.VMEM((16, 16, 256), BF16),
            dma((5,)), dma((16,)), dma((16,)), dma((8,)), dma((8,)),
            dma((7,)), dma((7,)), dma((7,)), dma((7,)), dma, dma,
        ],
        compiler_params=pltpu.CompilerParams(
            collective_id=0, has_side_effects=True, vmem_limit_bytes=40 * 1024 * 1024
        ),
    )(basis, gain, value, out)


def sum_factor(part_ref, whole_ref, part_b, slots, rs_send, rs_recv, ag_send, ag_recv):
    at = Place()
    greet([at.dp_peer(k) for k in range(1, 16)])
    piece = reduce_pieces(at, part_ref, part_b, slots, rs_send, rs_recv)
    own = whole_ref.at[piece_of(at.d)]
    own[...] = piece.astype(BF16)
    copies = [send(own, own, ag_send.at[k], ag_recv.at[k], at.dp_peer(k)) for k in range(1, 16)]
    for copy in copies:
        copy.wait()


def run_sum(part):
    vmem = pl.BlockSpec(memory_space=pltpu.VMEM)
    dma = pltpu.SemaphoreType.DMA
    return pl.pallas_call(
        sum_factor,
        out_shape=jax.ShapeDtypeStruct((16, 16, 256), BF16),
        in_specs=[vmem],
        out_specs=vmem,
        scratch_shapes=[
            pltpu.VMEM((16, 16, 256), BF16),
            pltpu.VMEM((16, 16, 256), BF16),
            dma((16,)), dma((16,)), dma((16,)), dma((16,)),
        ],
        compiler_params=pltpu.CompilerParams(collective_id=1, has_side_effects=True),
    )(part)


def chain(width, n_ref, gram_ref, c_ref, cot_ref, seg_ref, f_ref, xs, ps, es, hs, invs):
    sections = 16
    micros = c_ref.shape[0]
    gram = gram_ref[...]
    gram_b = gram.astype(BF16)
    mixings = [mixing_pair(seg_ref[m : m + 1, :].astype(F32)) for m in range(micros)]
    cs = [c_ref[m].astype(F32) for m in range(micros)]
    hh = [mm(c_ref[m], gram_b) for m in range(micros)]
    for s in range(sections):
        n = step_of(n_ref, s)
        ng = mm(n, gram_b).astype(BF16)
        for m in range(micros):
            cb = cs[m].astype(BF16)
            ms = jnp.sum(cs[m] * hh[m], axis=1, keepdims=True) * (1.0 / width)
            inv = lax.rsqrt(jnp.maximum(ms, 0.0) + EPS)
            e = mm(cb, n)
            f = mm(cb, ng)
            xs[s, m] = (inv * cs[m]).astype(BF16)
            es[s, m] = e
            hs[s, m] = hh[m]
            invs[s, m] = jnp.broadcast_to(inv, invs.shape[2:])
            y = mm(mixings[m][0], (inv * e).astype(BF16))
            z = mm(mixings[m][0], (inv * f).astype(BF16))
            cs[m] = cs[m] + y
            hh[m] = hh[m] + z
    gs = [cot_ref[m].astype(F32) for m in range(micros)]
    for s in reversed(range(sections)):
        n = step_of(n_ref, s)
        for m in range(micros):
            p = mm(mixings[m][1], gs[m].astype(BF16))
            pb = p.astype(BF16)
            ps[s, m] = pb
            q = mm(pb, n, ((1,), (1,)))
            inv = invs[s, m][:, :1]
            t = jnp.sum(p * es[s, m], axis=1, keepdims=True)
            gs[m] = gs[m] + inv * q - (inv * inv * inv * t * (1.0 / width)) * hs[s, m]
    own = lax.axis_index("section")
    total = mm(xs[own, 0], ps[own, 0], ((0,), (0,)))
    for m in range(1, micros):
        total = total + mm(xs[own, m], ps[own, m], ((0,), (0,)))
    f_ref[...] = total


def step_of(n_ref, s):
    z, xl = s // 2, s % 2
    return n_ref[:, z % 2, :, :, xl, z // 2].reshape(256, 256)


def run_chain(n_all, gram, coeffs, cotangent, segments, width):
    sections, sub = 16, 256
    micros, rows, _ = coeffs.shape
    whole = pl.BlockSpec(memory_space=pltpu.VMEM)
    return pl.pallas_call(
        functools.partial(chain, width),
        out_shape=jax.ShapeDtypeStruct((sub, sub), F32),
        in_specs=[whole] * 5,
        out_specs=whole,
        scratch_shapes=[
            pltpu.VMEM((sections, micros, rows, sub), BF16),
            pltpu.VMEM((sections, micros, rows, sub), BF16),
            pltpu.VMEM((sections, micros, rows, sub), F32),
            pltpu.VMEM((sections, micros, rows, sub), F32),
            pltpu.VMEM((sections, micros, rows, 128), F32),
        ],
        compiler_params=pltpu.CompilerParams(vmem_limit_bytes=48 * 1024 * 1024),
    )(n_all, gram, coeffs, cotangent, segments)


def finish(factor_ref, folded_ref, gain_ref, basis_hbm, value_hbm, out_hbm, gv_ref, go_ref, gg_ref,
           basis, value, out, gain_pad, go_wide, load_sem):
    d = lax.axis_index("dp")
    rows = pl.ds(pl.multiple_of(d * 256, 256), 256)
    loads = [
        pltpu.make_async_copy(out_hbm.at[0], out, load_sem.at[0]),
        pltpu.make_async_copy(basis_hbm.at[rows, :], basis, load_sem.at[1]),
        pltpu.make_async_copy(value_hbm.at[0, rows, :], value, load_sem.at[2]),
    ]
    for load in loads:
        load.start()
    factor = factor_ref[...].reshape(256, 256)
    go_wide[...] = mm(folded_ref[...], factor, ((0,), (0,)))
    go_ref[0] = go_wide[pl.ds(pl.multiple_of((d % 2) * 64, 64), 64), :]
    gain_pad[...] = jnp.zeros_like(gain_pad)
    gain_pad[0:16, :] = gain_ref[...]
    gain_cols = gain_pad[...].T
    lane = lax.broadcasted_iota(jnp.int32, gain_cols.shape, 1)
    own_gain = jnp.sum(jnp.where(lane == d, gain_cols, 0.0), axis=1, keepdims=True)
    loads[0].wait()
    loads[1].wait()
    left = mm(basis[...], factor).astype(BF16)
    plain = mm(left, out[...], ((1,), (1,)))
    gv_ref[0] = own_gain * plain
    loads[2].wait()
    sums = jnp.sum(plain * value[...].astype(F32), axis=1, keepdims=True)
    gg_ref[...] = jnp.broadcast_to(sums, (256, 128)).T[0:1, :]


def run_finish(factor, folded, gain, basis, value, out):
    vmem = pl.BlockSpec(memory_space=pltpu.VMEM)
    anywhere = pl.BlockSpec(memory_space=pl.ANY)
    return pl.pallas_call(
        finish,
        out_shape=(
            jax.ShapeDtypeStruct((1, 256, 1024), F32),
            jax.ShapeDtypeStruct((1, 64, 256), F32),
            jax.ShapeDtypeStruct((1, 256), F32),
        ),
        in_specs=[vmem, vmem, vmem, anywhere, anywhere, anywhere],
        out_specs=(vmem, vmem, vmem),
        scratch_shapes=[
            pltpu.VMEM((256, 256), BF16),
            pltpu.VMEM((256, 1024), BF16),
            pltpu.VMEM((1024, 256), BF16),
            pltpu.VMEM((128, 256), F32),
            pltpu.VMEM((128, 256), F32),
            pltpu.SemaphoreType.DMA((3,)),
        ],
        compiler_params=pltpu.CompilerParams(vmem_limit_bytes=24 * 1024 * 1024),
    )(factor, folded, gain, basis, value, out)


def shards(coeffs, cotangent, segment_ids, basis_matrix, section_gains, value_weight, out_weight):
    width = basis_matrix.shape[0]
    gain = section_gains.reshape(16, 256)
    steps, gram, folded = run_fold(basis_matrix, gain, value_weight, out_weight)
    part = run_chain(steps, gram, coeffs, cotangent, segment_ids, width)
    order = jnp.reshape(part, (16, 16, 256))
    factor = run_sum(order)
    grad_value, grad_out, grad_gain = run_finish(
        factor, folded, gain, basis_matrix, value_weight, out_weight
    )
    return (grad_value, grad_out, grad_gain)


def solution(mesh):
    placed = (
        P(None, "dp", None),
        P(None, "dp", None),
        P(None, "dp"),
        P(),
        P("section", None),
        P("section", None, None),
        P("section", None, None),
    )
    return jax.shard_map(
        shards,
        mesh=mesh,
        in_specs=placed,
        out_specs=(P("section", "dp", None), P("section", "dp", None), P("section", "dp")),
        check_vma=False,
    )
```

```python
import jax
import jax.numpy as jnp
from jax import lax
from jax.experimental import pallas as pl
from jax.experimental.pallas import tpu as pltpu
from jax.sharding import PartitionSpec as P

EPS = 1e-05
MESH = pl.DeviceIdType.MESH
F32 = jnp.float32
BF16 = jnp.bfloat16
VMEM_LIMIT = 60 * 1024 * 1024


def mm(a, b, dims=((1,), (0,))):
    return lax.dot_general(a, b, (dims, ((), ())), preferred_element_type=F32)


def mixing_pair(seg_row):
    rows = seg_row.shape[1]
    across = jnp.broadcast_to(seg_row, (rows, rows))
    down = across.T
    i = lax.broadcasted_iota(jnp.int32, (rows, rows), 0)
    j = lax.broadcasted_iota(jnp.int32, (rows, rows), 1)
    same = across == down
    low = jnp.where(same & (j <= i), 1.0, 0.0).astype(F32)
    high = jnp.where(same & (i <= j), 1.0, 0.0).astype(F32)
    mixing = (low / jnp.sum(low, axis=1, keepdims=True)).astype(BF16)
    mixing_t = (high / jnp.sum(high, axis=0, keepdims=True)).astype(BF16)
    return mixing, mixing_t


class Place:
    def __init__(self):
        self.s = lax.axis_index("section")
        self.d = lax.axis_index("dp")
        self.z = self.s // 2
        self.xl = self.s % 2
        self.y = self.d // 4
        self.xh = (self.d // 2) % 2
        self.core = self.d % 2
        self.x = self.xh * 2 + self.xl

    def dp_peer(self, k):
        return (self.s, (self.d + k) % 16)

    def z_peer(self, k):
        return (((self.z + k) % 8) * 2 + self.xl, self.d)

    def y_peer(self, k):
        return (self.s, ((self.y + k) % 4) * 4 + self.xh * 2 + self.core)

    def x_peer(self, k):
        x = (self.x + k) % 4
        return (self.z * 2 + x % 2, self.y * 4 + (x // 2) * 2 + self.core)

    def core_peer(self):
        return (self.s, self.y * 4 + self.xh * 2 + (self.core + 1) % 2)


def piece_of(d):
    return (d % 2) * 8 + d // 2


def send(src, dst, send_sem, recv_sem, peer):
    copy = pltpu.make_async_remote_copy(
        src_ref=src, dst_ref=dst, send_sem=send_sem, recv_sem=recv_sem,
        device_id=peer, device_id_type=MESH,
    )
    copy.start()
    return copy


def far_first(at):
    hops = lambda o: min(o[0], 4 - o[0]) + 2 * o[1]
    offsets = [(y, xh, c) for y in range(4) for xh in range(2) for c in range(2) if (y, xh, c) != (0, 0, 0)]
    offsets.sort(key=lambda o: -hops(o))
    peers = []
    for y, xh, c in offsets:
        y_to, xh_to, c_to = (at.y + y) % 4, (at.xh + xh) % 2, (at.core + c) % 2
        peers.append(((at.s, y_to * 4 + xh_to * 2 + c_to), c_to * 8 + y_to * 2 + xh_to))
    return peers


def relay(
    basis_hbm, gain_ref, value_hbm, out_hbm, c_ref, cot_ref, seg_ref, gv_ref, go_ref, gg_ref,
    value, basis, out, scaled_t, step, gain_pad, every, xs, ps, es, hs, invs,
    part, part_b, slots, whole, go_wide,
    load_sem, z_send, z_recv, a_send, a_recv, b_send, b_recv, c_send, c_recv,
    rs_send, rs_recv, ag_send, ag_recv,
):
    at = Place()
    width = basis.shape[0]
    block = 512
    blocks = width // block
    loads = [
        pltpu.make_async_copy(basis_hbm, basis, load_sem.at[0]),
        pltpu.make_async_copy(out_hbm.at[0], out, load_sem.at[1]),
    ]
    for i in range(blocks):
        rows = pl.ds(i * block, block)
        loads.append(pltpu.make_async_copy(value_hbm.at[0, rows, :], value.at[rows, :], load_sem.at[2 + i]))
    for load in loads:
        load.start()
    barrier = pltpu.get_barrier_semaphore()
    peers = [at.z_peer(k) for k in (4, 3, 5, 2, 6, 1, 7)] + [at.dp_peer(k) for k in range(1, 16)]
    peers += [at.x_peer(1), at.x_peer(3)]
    for peer in peers:
        pl.semaphore_signal(barrier, inc=1, device_id=peer, device_id_type=MESH)

    gram = jnp.zeros((256, 256), F32)
    own_step = jnp.zeros((256, 256), F32)
    loads[0].wait()
    loads[1].wait()
    for i in range(blocks):
        lanes = slice(i * block, (i + 1) * block)
        chunk = basis[lanes, :]
        chunk_t = chunk.astype(F32).T
        gram = gram + mm(chunk_t.astype(BF16), chunk)
        scaled = (chunk_t * gain_ref[0:1, lanes]).astype(BF16)
        scaled_t[:, lanes] = scaled
        loads[2 + i].wait()
        through = mm(value[lanes, :], out[...]).astype(BF16)
        own_step = own_step + mm(scaled, through)
    step[...] = own_step.astype(BF16).reshape(16, 16, 256)
    own = every.at[at.core, at.z % 2, at.z // 2, at.y, at.xh, at.xl]
    own[...] = step[piece_of(at.d)]

    pl.semaphore_wait(barrier, len(peers))
    over_z = [send(own, own, z_send.at[k], z_recv.at[k], at.z_peer(k)) for k in (4, 3, 5, 2, 6, 1, 7)]

    gram_b = gram.astype(BF16)
    for i in range(16):
        gain_pad[i : i + 1, :] = gain_ref[0:1, i * 256 : (i + 1) * 256]
    gain_pad[16:128, :] = jnp.zeros((112, 256), F32)
    gain_cols = gain_pad[...].T
    lane = lax.broadcasted_iota(jnp.int32, gain_cols.shape, 1)
    own_gain = jnp.sum(jnp.where(lane == at.d, gain_cols, 0.0), axis=1, keepdims=True)
    cols = pl.ds(pl.multiple_of((at.d // 2) * 128, 128), 128)
    folded = mm(scaled_t[...], value[:, cols]).astype(BF16)
    micros = c_ref.shape[0]
    mixings = [mixing_pair(seg_ref[m : m + 1, :].astype(F32)) for m in range(micros)]
    cs = [c_ref[m].astype(F32) for m in range(micros)]
    hh = [mm(c_ref[m], gram_b) for m in range(micros)]

    for copy in over_z:
        copy.wait_recv()
    own0 = every.at[at.core, 0, :, at.y, at.xh, at.xl]
    own1 = every.at[at.core, 1, :, at.y, at.xh, at.xl]
    first = []
    for k in (2, 1, 3):
        first.append(send(own0, own0, a_send.at[0, k], a_recv.at[0, k], at.x_peer(k)))
        first.append(send(own1, own1, a_send.at[1, k], a_recv.at[1, k], at.y_peer(k)))
    for copy in first:
        copy.wait_recv()
    second = []
    for q in range(4):
        row0 = every.at[at.core, 0, q, at.y]
        row1 = every.at[at.core, 1, q, :, at.xh, at.xl]
        group = []
        for k in (2, 1, 3):
            group.append(send(row0, row0, b_send.at[0, q, k], b_recv.at[0, q, k], at.y_peer(k)))
            group.append(send(row1, row1, b_send.at[1, q, k], b_recv.at[1, q, k], at.x_peer(k)))
        second.append(group)
    across = []

    def land(q):
        for copy in second[q]:
            copy.wait_recv()
        half = every.at[at.core, :, q]
        across.append(send(half, half, c_send.at[q], c_recv.at[q], at.core_peer()))

    def step_of(s):
        z, xl = s // 2, s % 2
        return every[:, z % 2, z // 2, :, :, xl].reshape(256, 256)

    def forward(s):
        n = step_of(s)
        ng = mm(n, gram_b).astype(BF16)
        for m in range(micros):
            cb = cs[m].astype(BF16)
            ms = jnp.sum(cs[m] * hh[m], axis=1, keepdims=True) * (1.0 / width)
            inv = lax.rsqrt(jnp.maximum(ms, 0.0) + EPS)
            e = mm(cb, n)
            xs[s, m] = (inv * cs[m]).astype(BF16)
            es[s, m] = e
            hs[s, m] = hh[m]
            invs[s, m] = jnp.broadcast_to(inv, invs.shape[2:])
            if s < 15:
                f = mm(cb, ng)
                cs[m] = cs[m] + mm(mixings[m][0], (inv * e).astype(BF16))
                hh[m] = hh[m] + mm(mixings[m][0], (inv * f).astype(BF16))

    land(0)
    across[0].wait_recv()
    for q in range(4):
        forward(4 * q)
        forward(4 * q + 1)
        if q < 3:
            land(q + 1)
        forward(4 * q + 2)
        forward(4 * q + 3)
        if q < 3:
            across[q + 1].wait_recv()

    gs = [cot_ref[m].astype(F32) for m in range(micros)]
    for s in reversed(range(16)):
        n = step_of(s)
        for m in range(micros):
            p = mm(mixings[m][1], gs[m].astype(BF16))
            pb = p.astype(BF16)
            ps[s, m] = pb
            if s > 0:
                q = mm(pb, n, ((1,), (1,)))
                inv = invs[s, m][:, :1]
                t = jnp.sum(p * es[s, m], axis=1, keepdims=True)
                gs[m] = gs[m] + inv * q - (inv * inv * inv * t * (1.0 / width)) * hs[s, m]

    total = mm(xs[at.s, 0], ps[at.s, 0], ((0,), (0,)))
    for m in range(1, micros):
        total = total + mm(xs[at.s, m], ps[at.s, m], ((0,), (0,)))
    part[...] = total.reshape(16, 16, 256)
    part_b[...] = total.astype(BF16).reshape(16, 16, 256)
    others = far_first(at)
    pieces = [
        send(part_b.at[piece], slots.at[i], rs_send.at[i], rs_recv.at[i], peer)
        for i, (peer, piece) in enumerate(others)
    ]
    mine = part[piece_of(at.d)]
    for i in reversed(range(15)):
        pieces[i].wait_recv()
        mine = mine + slots[i].astype(F32)
    summed = whole.at[piece_of(at.d)]
    summed[...] = mine.astype(BF16)
    spread = [
        send(summed, summed, ag_send.at[i], ag_recv.at[i], peer) for i, (peer, piece) in enumerate(others)
    ]
    for copy in spread:
        copy.wait_recv()

    factor = whole[...].reshape(256, 256)
    own_rows = pl.ds(pl.multiple_of(at.d * 256, 256), 256)
    left = mm(basis[own_rows, :], factor).astype(BF16)
    plain = mm(left, out[...], ((1,), (1,)))
    gv_ref[0] = own_gain * plain
    go_wide[...] = mm(folded, factor, ((0,), (0,)))
    go_ref[0] = go_wide[pl.ds(pl.multiple_of((at.d % 2) * 64, 64), 64), :]
    sums = jnp.sum(plain * value[own_rows, :].astype(F32), axis=1, keepdims=True)
    gg_ref[...] = jnp.broadcast_to(sums, (256, 128)).T[0:1, :]
    for copy in over_z + first + sum(second, []) + across + pieces + spread:
        copy.wait_send()


def shards(coeffs, cotangent, segment_ids, basis_matrix, section_gains, value_weight, out_weight):
    vmem = pl.BlockSpec(memory_space=pltpu.VMEM)
    anywhere = pl.BlockSpec(memory_space=pl.ANY)
    dma = pltpu.SemaphoreType.DMA
    return pl.pallas_call(
        relay,
        out_shape=(
            jax.ShapeDtypeStruct((1, 256, 1024), F32),
            jax.ShapeDtypeStruct((1, 64, 256), F32),
            jax.ShapeDtypeStruct((1, 256), F32),
        ),
        in_specs=[anywhere, vmem, anywhere, anywhere, vmem, vmem, vmem],
        out_specs=(vmem, vmem, vmem),
        scratch_shapes=[
            pltpu.VMEM((4096, 1024), BF16),
            pltpu.VMEM((4096, 256), BF16),
            pltpu.VMEM((1024, 256), BF16),
            pltpu.VMEM((256, 4096), BF16),
            pltpu.VMEM((16, 16, 256), BF16),
            pltpu.VMEM((128, 256), F32),
            pltpu.VMEM((2, 2, 4, 4, 2, 2, 16, 256), BF16),
            pltpu.VMEM((16, 2, 128, 256), BF16),
            pltpu.VMEM((16, 2, 128, 256), BF16),
            pltpu.VMEM((16, 2, 128, 256), F32),
            pltpu.VMEM((16, 2, 128, 256), F32),
            pltpu.VMEM((16, 2, 128, 128), F32),
            pltpu.VMEM((16, 16, 256), F32),
            pltpu.VMEM((16, 16, 256), BF16),
            pltpu.VMEM((15, 16, 256), BF16),
            pltpu.VMEM((16, 16, 256), BF16),
            pltpu.VMEM((128, 256), F32),
            dma((10,)), dma((8,)), dma((8,)), dma((2, 4)), dma((2, 4)),
            dma((2, 4, 4)), dma((2, 4, 4)), dma((4,)), dma((4,)),
            dma((15,)), dma((15,)), dma((15,)), dma((15,)),
        ],
        compiler_params=pltpu.CompilerParams(
            collective_id=0, has_side_effects=True, vmem_limit_bytes=VMEM_LIMIT
        ),
    )(basis_matrix, section_gains, value_weight, out_weight, coeffs, cotangent, segment_ids)


def solution(mesh):
    placed = (
        P(None, "dp", None),
        P(None, "dp", None),
        P(None, "dp"),
        P(),
        P("section", None),
        P("section", None, None),
        P("section", None, None),
    )
    return jax.shard_map(
        shards,
        mesh=mesh,
        in_specs=placed,
        out_specs=(P("section", "dp", None), P("section", "dp", None), P("section", "dp")),
        check_vma=False,
    )
```

```python
import jax
import jax.numpy as jnp
from jax import lax
from jax.experimental import pallas as pl
from jax.experimental.pallas import tpu as pltpu
from jax.sharding import PartitionSpec as P

EPS = 1e-05
MESH = pl.DeviceIdType.MESH
F32 = jnp.float32
BF16 = jnp.bfloat16
VMEM_LIMIT = 58 * 1024 * 1024


def mm(a, b, dims=((1,), (0,))):
    return lax.dot_general(a, b, (dims, ((), ())), preferred_element_type=F32)


def mixing_pair(seg_row):
    rows = seg_row.shape[1]
    across = jnp.broadcast_to(seg_row, (rows, rows))
    down = across.T
    i = lax.broadcasted_iota(jnp.int32, (rows, rows), 0)
    j = lax.broadcasted_iota(jnp.int32, (rows, rows), 1)
    same = across == down
    low = jnp.where(same & (j <= i), 1.0, 0.0).astype(F32)
    high = jnp.where(same & (i <= j), 1.0, 0.0).astype(F32)
    mixing = (low / jnp.sum(low, axis=1, keepdims=True)).astype(BF16)
    mixing_t = (high / jnp.sum(high, axis=0, keepdims=True)).astype(BF16)
    return mixing, mixing_t


class Place:
    def __init__(self):
        self.s = lax.axis_index("section")
        self.d = lax.axis_index("dp")
        self.z = self.s // 2
        self.xl = self.s % 2
        self.y = self.d // 4
        self.xh = (self.d // 2) % 2
        self.core = self.d % 2
        self.x = self.xh * 2 + self.xl

    def dp_peer(self, k):
        return (self.s, (self.d + k) % 16)

    def z_peer(self, k):
        return (((self.z + k) % 8) * 2 + self.xl, self.d)

    def y_peer(self, k):
        return (self.s, ((self.y + k) % 4) * 4 + self.xh * 2 + self.core)

    def x_peer(self, k):
        x = (self.x + k) % 4
        return (self.z * 2 + x % 2, self.y * 4 + (x // 2) * 2 + self.core)

    def core_peer(self):
        return (self.s, self.y * 4 + self.xh * 2 + (self.core + 1) % 2)


def piece_of(d):
    return (d % 2) * 8 + d // 2


def send(src, dst, send_sem, recv_sem, peer):
    copy = pltpu.make_async_remote_copy(
        src_ref=src, dst_ref=dst, send_sem=send_sem, recv_sem=recv_sem,
        device_id=peer, device_id_type=MESH,
    )
    copy.start()
    return copy


def far_first(at):
    hops = lambda o: min(o[0], 4 - o[0]) + 2 * o[1]
    offsets = [(y, xh, c) for y in range(4) for xh in range(2) for c in range(2) if (y, xh, c) != (0, 0, 0)]
    offsets.sort(key=lambda o: -hops(o))
    peers = []
    for y, xh, c in offsets:
        y_to, xh_to, c_to = (at.y + y) % 4, (at.xh + xh) % 2, (at.core + c) % 2
        peers.append(((at.s, y_to * 4 + xh_to * 2 + c_to), c_to * 8 + y_to * 2 + xh_to))
    return peers


def relay(
    basis_hbm, gain_hbm, value_hbm, out_hbm, c_hbm, cot_hbm, seg_hbm,
    whole, folded_ref, own_gain_ref,
    out, value, value_cols, basis_half, basis, gain_half, gain, c_ref, cot_ref, seg_ref,
    part_n, part_nb, slot_n, gain_pad, every, xs, ps, es, hs, invs, part, part_b, slots,
    load_sem, n_send, n_recv, z_send, z_recv, y_send, y_recv, x_send, x_recv, c_send, c_recv,
    rs_send, rs_recv, ag_send, ag_recv,
):
    at = Place()
    width = basis.shape[0]
    half = width // 2
    cuts = (0, 512, 1024, 2048)
    start = pl.multiple_of(at.core * half, half)

    def load(i, src, dst):
        copy = pltpu.make_async_copy(src, dst, load_sem.at[i])
        copy.start()
        return copy

    early = [
        load(0, gain_hbm.at[:, pl.ds(start, half)], gain_half),
        load(1, basis_hbm.at[pl.ds(start, half), :], basis_half),
        load(2, out_hbm.at[0], out),
    ]
    for i in range(3):
        size = cuts[i + 1] - cuts[i]
        rows = pl.ds(pl.multiple_of(start + cuts[i], 512), size)
        early.append(load(3 + i, value_hbm.at[0, rows, :], value.at[pl.ds(cuts[i], size), :]))
    barrier = pltpu.get_barrier_semaphore()
    peers = [at.z_peer(k) for k in (4, 3, 5, 2, 6, 1, 7)] + [at.dp_peer(k) for k in range(1, 16)]
    peers += [at.x_peer(1), at.x_peer(3)]
    for peer in peers:
        pl.semaphore_signal(barrier, inc=1, device_id=peer, device_id_type=MESH)
    cols = pl.ds(pl.multiple_of((at.d // 2) * 128, 128), 128)
    late = [
        load(6, basis_hbm, basis),
        load(7, value_hbm.at[0, :, cols], value_cols),
        load(8, gain_hbm, gain),
        load(9, c_hbm, c_ref),
        load(10, seg_hbm, seg_ref),
        load(11, cot_hbm, cot_ref),
    ]

    partial = jnp.zeros((256, 256), F32)
    for copy in early[:3]:
        copy.wait()
    for i in range(3):
        lanes = slice(cuts[i], cuts[i + 1])
        scaled = (basis_half[lanes, :].astype(F32).T * gain_half[0:1, lanes]).astype(BF16)
        early[3 + i].wait()
        through = mm(value[lanes, :], out[...]).astype(BF16)
        partial = partial + mm(scaled, through)
    part_n[...] = partial.reshape(8, 32, 256)
    part_nb[...] = partial.astype(BF16).reshape(8, 32, 256)

    pl.semaphore_wait(barrier, len(peers))
    other = (at.core + 1) % 2
    swap = send(part_nb.at[other * 4 + at.y], slot_n, n_send, n_recv, at.core_peer())
    swap.wait_recv()
    own = every.at[at.core, at.z // 2, at.xl, at.z % 2, at.y]
    own[...] = (part_n[at.core * 4 + at.y] + slot_n[...].astype(F32)).astype(BF16)
    over_z = [send(own, own, z_send.at[k], z_recv.at[k], at.z_peer(k)) for k in (4, 3, 5, 2, 6, 1, 7)]

    for copy in late:
        copy.wait()
    gram = jnp.zeros((256, 256), F32)
    folded = jnp.zeros((256, 128), F32)
    for i in range(8):
        lanes = slice(i * 512, (i + 1) * 512)
        chunk = basis[lanes, :]
        chunk_t = chunk.astype(F32).T
        gram = gram + mm(chunk_t.astype(BF16), chunk)
        scaled = (chunk_t * gain[0:1, lanes]).astype(BF16)
        folded = folded + mm(scaled, value_cols[lanes, :])
    folded_ref[...] = folded.astype(BF16)
    gram_b = gram.astype(BF16)
    for i in range(16):
        gain_pad[i : i + 1, :] = gain[0:1, i * 256 : (i + 1) * 256]
    gain_pad[16:128, :] = jnp.zeros((112, 256), F32)
    gain_cols = gain_pad[...].T
    lane = lax.broadcasted_iota(jnp.int32, gain_cols.shape, 1)
    own_gain = jnp.sum(jnp.where(lane == at.d, gain_cols, 0.0), axis=1, keepdims=True)
    own_gain_ref[...] = jnp.broadcast_to(own_gain, own_gain_ref.shape)
    micros = c_ref.shape[0]
    mixings = [mixing_pair(seg_ref[m : m + 1, :].astype(F32)) for m in range(micros)]
    cs = [c_ref[m].astype(F32) for m in range(micros)]
    hh = [mm(c_ref[m], gram_b) for m in range(micros)]

    for copy in over_z:
        copy.wait_recv()
    over_y = []
    for q in range(4):
        mine = every.at[at.core, q, at.xl, :, at.y]
        over_y.append(
            [send(mine, mine, y_send.at[q, k], y_recv.at[q, k], at.y_peer(k)) for k in (2, 1, 3)]
        )
    over_x, across = [], []

    def pass_x(q):
        for copy in over_y[q]:
            copy.wait_recv()
        low = every.at[at.core, q, at.xl, :, pl.ds(0, 2)]
        high = every.at[at.core, q, at.xl, :, pl.ds(2, 2)]
        over_x.append([
            send(low, low, x_send.at[q, 0], x_recv.at[q, 0], at.x_peer(1)),
            send(high, high, x_send.at[q, 1], x_recv.at[q, 1], at.x_peer(3)),
        ])

    def pass_core(q):
        for copy in over_x[q]:
            copy.wait_recv()
        chunk = every.at[at.core, q]
        across.append(send(chunk, chunk, c_send.at[q], c_recv.at[q], at.core_peer()))

    def step_of(s):
        z, xl = s // 2, s % 2
        return every[:, z // 2, xl, z % 2].reshape(256, 256)

    def onward(s):
        return mm(step_of(s), gram_b).astype(BF16)

    def forward(s, ng):
        n = step_of(s)
        both = range(micros)
        es_ = [mm(cs[m].astype(BF16), n) for m in both]
        invs_ = []
        for m in both:
            ms = jnp.sum(cs[m] * hh[m], axis=1, keepdims=True) * (1.0 / width)
            invs_.append(lax.rsqrt(jnp.maximum(ms, 0.0) + EPS))
        fs_ = [mm(cs[m].astype(BF16), ng) for m in both] if s < 15 else []
        old = list(cs)
        for m in both:
            xs[s, m] = (invs_[m] * old[m]).astype(BF16)
            es[s, m] = es_[m]
            hs[s, m] = hh[m]
            invs[s, m] = jnp.broadcast_to(invs_[m], invs.shape[2:])
        if s == 15:
            return None
        ys_ = [mm(mixings[m][0], (invs_[m] * es_[m]).astype(BF16)) for m in both]
        for m in both:
            cs[m] = cs[m] + ys_[m]
        ng = onward(s + 1)
        zs_ = [mm(mixings[m][0], (invs_[m] * fs_[m]).astype(BF16)) for m in both]
        for m in both:
            hh[m] = hh[m] + zs_[m]
        return ng

    pass_x(0)
    pass_x(1)
    pass_core(0)
    pass_x(2)
    pass_core(1)
    across[0].wait_recv()
    ng = onward(0)
    ng = forward(0, ng)
    ng = forward(1, ng)
    pass_x(3)
    ng = forward(2, ng)
    pass_core(2)
    across[1].wait_recv()
    for s in (3, 4, 5):
        ng = forward(s, ng)
    pass_core(3)
    ng = forward(6, ng)
    across[2].wait_recv()
    for s in (7, 8, 9, 10):
        ng = forward(s, ng)
    across[3].wait_recv()
    for s in (11, 12, 13, 14, 15):
        ng = forward(s, ng)

    gs = [cot_ref[m].astype(F32) for m in range(micros)]
    for s in reversed(range(16)):
        n = step_of(s)
        both = range(micros)
        ps_ = [mm(mixings[m][1], gs[m].astype(BF16)) for m in both]
        pb_ = [p.astype(BF16) for p in ps_]
        qs_ = [mm(p, n, ((1,), (1,))) for p in pb_] if s > 0 else []
        for m in both:
            ps[s, m] = pb_[m]
            if s > 0:
                inv = invs[s, m][:, :1]
                t = jnp.sum(ps_[m] * es[s, m], axis=1, keepdims=True)
                gs[m] = (gs[m] - (inv * inv * inv * t * (1.0 / width)) * hs[s, m]) + inv * qs_[m]

    rows = micros * xs.shape[2]
    total = mm(xs[at.s].reshape(rows, 256), ps[at.s].reshape(rows, 256), ((0,), (0,)))
    part[...] = total.reshape(16, 16, 256)
    part_b[...] = total.astype(BF16).reshape(16, 16, 256)
    others = far_first(at)
    pieces = [
        send(part_b.at[piece], slots.at[i], rs_send.at[i], rs_recv.at[i], peer)
        for i, (peer, piece) in enumerate(others)
    ]
    mine = part[piece_of(at.d)]
    for i in reversed(range(15)):
        pieces[i].wait_recv()
        mine = mine + slots[i].astype(F32)
    summed = whole.at[piece_of(at.d)]
    summed[...] = mine.astype(BF16)
    spread = [
        send(summed, summed, ag_send.at[i], ag_recv.at[i], peer) for i, (peer, piece) in enumerate(others)
    ]
    for copy in [swap] + over_z + sum(over_y, []) + sum(over_x, []) + across + pieces:
        copy.wait_send()
    for copy in spread:
        copy.wait()


def finish(factor_hbm, folded_hbm, own_gain_hbm, out_hbm, basis_hbm, value_hbm, gv_hbm, go_hbm, gg_hbm,
           factor_ref, folded, own_gain, out, basis, value, gv, go, gg, load_sem, store_sem):
    d = lax.axis_index("dp")
    rows = pl.ds(pl.multiple_of(d * 256, 256), 256)
    loads = [
        pltpu.make_async_copy(factor_hbm, factor_ref, load_sem.at[0]),
        pltpu.make_async_copy(basis_hbm.at[rows, :], basis, load_sem.at[1]),
        pltpu.make_async_copy(out_hbm.at[0], out, load_sem.at[2]),
        pltpu.make_async_copy(own_gain_hbm, own_gain, load_sem.at[3]),
        pltpu.make_async_copy(value_hbm.at[0, rows, :], value, load_sem.at[4]),
        pltpu.make_async_copy(folded_hbm, folded, load_sem.at[5]),
    ]
    for load in loads:
        load.start()
    for load in loads:
        load.wait()
    factor = factor_ref[...].reshape(256, 256)
    left = mm(basis[...], factor).astype(BF16)
    gain = own_gain[:, :1]
    sums = jnp.zeros((256, 1), F32)
    stores = []
    for i in range(4):
        lanes = slice(i * 256, (i + 1) * 256)
        plain = mm(left, out[lanes, :], ((1,), (1,)))
        gv[:, lanes] = gain * plain
        stores.append(pltpu.make_async_copy(
            gv.at[:, lanes], gv_hbm.at[0, :, lanes], store_sem.at[i]))
        stores[-1].start()
        sums = sums + jnp.sum(plain * value[:, lanes].astype(F32), axis=1, keepdims=True)
    go[...] = mm(folded[...], factor, ((0,), (0,)))
    own = pl.ds(pl.multiple_of((d % 2) * 64, 64), 64)
    stores.append(pltpu.make_async_copy(go.at[own, :], go_hbm.at[0], store_sem.at[4]))
    stores[-1].start()
    gg[...] = jnp.broadcast_to(sums, (256, 128)).T[0:1, :]
    stores.append(pltpu.make_async_copy(gg, gg_hbm, store_sem.at[5]))
    stores[-1].start()
    for store in stores:
        store.wait()


def shards(coeffs, cotangent, segment_ids, basis_matrix, section_gains, value_weight, out_weight):
    vmem = pl.BlockSpec(memory_space=pltpu.VMEM)
    hbm = pl.BlockSpec(memory_space=pltpu.HBM)
    dma = pltpu.SemaphoreType.DMA
    shape = jax.ShapeDtypeStruct
    handed = pl.pallas_call(
        relay,
        out_shape=(
            shape((16, 16, 256), BF16),
            shape((256, 128), BF16),
            shape((256, 128), F32),
        ),
        in_specs=[hbm] * 7,
        out_specs=(vmem,) * 3,
        scratch_shapes=[
            pltpu.VMEM((1024, 256), BF16),
            pltpu.VMEM((2048, 1024), BF16),
            pltpu.VMEM((4096, 128), BF16),
            pltpu.VMEM((2048, 256), BF16),
            pltpu.VMEM((4096, 256), BF16),
            pltpu.VMEM((1, 2048), F32),
            pltpu.VMEM((1, 4096), F32),
            pltpu.VMEM((2, 128, 256), BF16),
            pltpu.VMEM((2, 128, 256), BF16),
            pltpu.VMEM((2, 128), jnp.int32),
            pltpu.VMEM((8, 32, 256), F32),
            pltpu.VMEM((8, 32, 256), BF16),
            pltpu.VMEM((32, 256), BF16),
            pltpu.VMEM((128, 256), F32),
            pltpu.VMEM((2, 4, 2, 2, 4, 32, 256), BF16),
            pltpu.VMEM((16, 2, 128, 256), BF16),
            pltpu.VMEM((16, 2, 128, 256), BF16),
            pltpu.VMEM((16, 2, 128, 256), F32),
            pltpu.VMEM((16, 2, 128, 256), F32),
            pltpu.VMEM((16, 2, 128, 128), F32),
            pltpu.VMEM((16, 16, 256), F32),
            pltpu.VMEM((16, 16, 256), BF16),
            pltpu.VMEM((15, 16, 256), BF16),
            dma((12,)), dma, dma, dma((8,)), dma((8,)),
            dma((4, 4)), dma((4, 4)), dma((4, 2)), dma((4, 2)), dma((4,)), dma((4,)),
            dma((15,)), dma((15,)), dma((15,)), dma((15,)),
        ],
        compiler_params=pltpu.CompilerParams(
            collective_id=0, has_side_effects=True, vmem_limit_bytes=VMEM_LIMIT
        ),
    )(basis_matrix, section_gains, value_weight, out_weight, coeffs, cotangent, segment_ids)
    return pl.pallas_call(
        finish,
        out_shape=(
            shape((1, 256, 1024), F32),
            shape((1, 64, 256), F32),
            shape((1, 256), F32),
        ),
        in_specs=[hbm] * 6,
        out_specs=(hbm,) * 3,
        scratch_shapes=[
            pltpu.VMEM((16, 16, 256), BF16),
            pltpu.VMEM((256, 128), BF16),
            pltpu.VMEM((256, 128), F32),
            pltpu.VMEM((1024, 256), BF16),
            pltpu.VMEM((256, 256), BF16),
            pltpu.VMEM((256, 1024), BF16),
            pltpu.VMEM((256, 1024), F32),
            pltpu.VMEM((128, 256), F32),
            pltpu.VMEM((1, 256), F32),
            dma((6,)),
            dma((6,)),
        ],
        compiler_params=pltpu.CompilerParams(vmem_limit_bytes=VMEM_LIMIT),
    )(*handed, out_weight, basis_matrix, value_weight)


def solution(mesh):
    placed = (
        P(None, "dp", None),
        P(None, "dp", None),
        P(None, "dp"),
        P(),
        P("section", None),
        P("section", None, None),
        P("section", None, None),
    )
    return jax.shard_map(
        shards,
        mesh=mesh,
        in_specs=placed,
        out_specs=(P("section", "dp", None), P("section", "dp", None), P("section", "dp")),
        check_vma=False,
    )
```

```python
import jax
import jax.numpy as jnp
from jax import lax
from jax.experimental import pallas as pl
from jax.experimental.pallas import tpu as pltpu
from jax.sharding import PartitionSpec as P

EPS = 1e-05
MESH = pl.DeviceIdType.MESH
F32 = jnp.float32
BF16 = jnp.bfloat16
VMEM_LIMIT = 58 * 1024 * 1024


def mm(a, b, dims=((1,), (0,))):
    return lax.dot_general(a, b, (dims, ((), ())), preferred_element_type=F32)


def mixing_pair(seg_row):
    rows = seg_row.shape[1]
    across = jnp.broadcast_to(seg_row, (rows, rows))
    down = across.T
    i = lax.broadcasted_iota(jnp.int32, (rows, rows), 0)
    j = lax.broadcasted_iota(jnp.int32, (rows, rows), 1)
    same = across == down
    low = jnp.where(same & (j <= i), 1.0, 0.0).astype(F32)
    high = jnp.where(same & (i <= j), 1.0, 0.0).astype(F32)
    mixing = (low / jnp.sum(low, axis=1, keepdims=True)).astype(BF16)
    mixing_t = (high / jnp.sum(high, axis=0, keepdims=True)).astype(BF16)
    return mixing, mixing_t


class Place:
    def __init__(self):
        self.s = lax.axis_index("section")
        self.d = lax.axis_index("dp")
        self.z = self.s // 2
        self.xl = self.s % 2
        self.y = self.d // 4
        self.xh = (self.d // 2) % 2
        self.core = self.d % 2
        self.x = self.xh * 2 + self.xl

    def dp_peer(self, k):
        return (self.s, (self.d + k) % 16)

    def z_peer(self, k):
        return (((self.z + k) % 8) * 2 + self.xl, self.d)

    def y_peer(self, k):
        return (self.s, ((self.y + k) % 4) * 4 + self.xh * 2 + self.core)

    def x_peer(self, k):
        x = (self.x + k) % 4
        return (self.z * 2 + x % 2, self.y * 4 + (x // 2) * 2 + self.core)

    def core_peer(self):
        return (self.s, self.y * 4 + self.xh * 2 + (self.core + 1) % 2)


def piece_of(d):
    return (d % 2) * 8 + d // 2


def send(src, dst, send_sem, recv_sem, peer):
    copy = pltpu.make_async_remote_copy(
        src_ref=src, dst_ref=dst, send_sem=send_sem, recv_sem=recv_sem,
        device_id=peer, device_id_type=MESH,
    )
    copy.start()
    return copy


def far_first(at):
    hops = lambda o: min(o[0], 4 - o[0]) + 2 * o[1]
    offsets = [(y, xh, c) for y in range(4) for xh in range(2) for c in range(2) if (y, xh, c) != (0, 0, 0)]
    offsets.sort(key=lambda o: -hops(o))
    peers = []
    for y, xh, c in offsets:
        y_to, xh_to, c_to = (at.y + y) % 4, (at.xh + xh) % 2, (at.core + c) % 2
        peers.append(((at.s, y_to * 4 + xh_to * 2 + c_to), c_to * 8 + y_to * 2 + xh_to))
    return peers


def relay(
    basis_hbm, gain_hbm, value_hbm, out_hbm, c_hbm, cot_hbm, seg_hbm,
    whole, folded_ref, own_gain_ref,
    out, value, value_cols, basis_half, basis, gain_half, gain, c_ref, cot_ref, seg_ref,
    part_n, part_nb, slot_n, gain_pad, every, xs, ps, es, hs, invs, part, part_b, slots,
    load_sem, n_send, n_recv, z_send, z_recv, y_send, y_recv, x_send, x_recv, c_send, c_recv,
    rs_send, rs_recv, ag_send, ag_recv,
):
    at = Place()
    width = basis.shape[0]
    half = width // 2
    cuts = (0, 512, 1024, 2048)
    start = pl.multiple_of(at.core * half, half)

    def load(i, src, dst):
        copy = pltpu.make_async_copy(src, dst, load_sem.at[i])
        copy.start()
        return copy

    early = [
        load(0, gain_hbm.at[:, pl.ds(start, half)], gain_half),
        load(1, basis_hbm.at[pl.ds(start, half), :], basis_half),
        load(2, out_hbm.at[0], out),
    ]
    for i in range(3):
        size = cuts[i + 1] - cuts[i]
        rows = pl.ds(pl.multiple_of(start + cuts[i], 512), size)
        early.append(load(3 + i, value_hbm.at[0, rows, :], value.at[pl.ds(cuts[i], size), :]))
    barrier = pltpu.get_barrier_semaphore()
    peers = [at.z_peer(k) for k in (4, 3, 5, 2, 6, 1, 7)] + [at.dp_peer(k) for k in range(1, 16)]
    peers += [at.x_peer(1), at.x_peer(3)]
    for peer in peers:
        pl.semaphore_signal(barrier, inc=1, device_id=peer, device_id_type=MESH)
    cols = pl.ds(pl.multiple_of((at.d // 2) * 128, 128), 128)
    late = [
        load(6, basis_hbm, basis),
        load(7, value_hbm.at[0, :, cols], value_cols),
        load(8, gain_hbm, gain),
        load(9, c_hbm, c_ref),
        load(10, seg_hbm, seg_ref),
        load(11, cot_hbm, cot_ref),
    ]

    partial = jnp.zeros((256, 256), F32)
    for copy in early[:3]:
        copy.wait()
    for i in range(3):
        lanes = slice(cuts[i], cuts[i + 1])
        scaled = (basis_half[lanes, :].astype(F32).T * gain_half[0:1, lanes]).astype(BF16)
        early[3 + i].wait()
        through = mm(value[lanes, :], out[...]).astype(BF16)
        partial = partial + mm(scaled, through)
    part_n[...] = partial.reshape(8, 32, 256)
    part_nb[...] = partial.astype(BF16).reshape(8, 32, 256)

    pl.semaphore_wait(barrier, len(peers))
    other = (at.core + 1) % 2
    swap = send(part_nb.at[other * 4 + at.y], slot_n, n_send, n_recv, at.core_peer())
    swap.wait_recv()
    own = every.at[at.core, at.z, at.xl, at.y]
    own[...] = (part_n[at.core * 4 + at.y] + slot_n[...].astype(F32)).astype(BF16)
    over_z = [send(own, own, z_send.at[k], z_recv.at[at.z], at.z_peer(k)) for k in (4, 3, 5, 2, 6, 1, 7)]

    for copy in late:
        copy.wait()
    gram = jnp.zeros((256, 256), F32)
    folded = jnp.zeros((256, 128), F32)
    for i in range(8):
        lanes = slice(i * 512, (i + 1) * 512)
        chunk = basis[lanes, :]
        chunk_t = chunk.astype(F32).T
        gram = gram + mm(chunk_t.astype(BF16), chunk)
        scaled = (chunk_t * gain[0:1, lanes]).astype(BF16)
        folded = folded + mm(scaled, value_cols[lanes, :])
    folded_ref[...] = folded.astype(BF16)
    gram_b = gram.astype(BF16)
    for i in range(16):
        gain_pad[i : i + 1, :] = gain[0:1, i * 256 : (i + 1) * 256]
    gain_pad[16:128, :] = jnp.zeros((112, 256), F32)
    gain_cols = gain_pad[...].T
    lane = lax.broadcasted_iota(jnp.int32, gain_cols.shape, 1)
    own_gain = jnp.sum(jnp.where(lane == at.d, gain_cols, 0.0), axis=1, keepdims=True)
    own_gain_ref[...] = jnp.broadcast_to(own_gain, own_gain_ref.shape)
    micros = c_ref.shape[0]
    mixings = [mixing_pair(seg_ref[m : m + 1, :].astype(F32)) for m in range(micros)]
    cs = [c_ref[m].astype(F32) for m in range(micros)]
    hh = [mm(c_ref[m], gram_b) for m in range(micros)]

    bounds = (0, 1, 2, 4, 6, 8)
    over_y, over_x, across = [], [], []

    def arrived(z):
        @pl.when(at.z != z)
        def _():
            there = every.at[at.core, z, at.xl, at.y]
            pltpu.make_async_remote_copy(
                src_ref=there, dst_ref=there, send_sem=z_send.at[0], recv_sem=z_recv.at[z],
                device_id=at.core_peer(), device_id_type=MESH,
            ).wait_recv()

    def planes(q):
        return pl.ds(bounds[q], bounds[q + 1] - bounds[q])

    def start_y(q):
        for z in range(bounds[q], bounds[q + 1]):
            arrived(z)
        mine = every.at[at.core, planes(q), at.xl, at.y]
        over_y.append(
            [send(mine, mine, y_send.at[q, k], y_recv.at[q, k], at.y_peer(k)) for k in (2, 1, 3)]
        )

    def start_x(q):
        for copy in over_y[q]:
            copy.wait_recv()
        low = every.at[at.core, planes(q), at.xl, pl.ds(0, 2)]
        high = every.at[at.core, planes(q), at.xl, pl.ds(2, 2)]
        over_x.append([
            send(low, low, x_send.at[q, 0], x_recv.at[q, 0], at.x_peer(1)),
            send(high, high, x_send.at[q, 1], x_recv.at[q, 1], at.x_peer(3)),
        ])

    def start_core(q):
        for copy in over_x[q]:
            copy.wait_recv()
        chunk = every.at[at.core, planes(q)]
        across.append(send(chunk, chunk, c_send.at[q], c_recv.at[q], at.core_peer()))

    def sent(copies):
        for copy in copies:
            copy.wait_send()

    def step_of(s):
        z, xl = s // 2, s % 2
        return every[:, z, xl].reshape(256, 256)

    def onward(s):
        return mm(step_of(s), gram_b).astype(BF16)

    def forward(s, ng):
        n = step_of(s)
        both = range(micros)
        es_ = [mm(cs[m].astype(BF16), n) for m in both]
        invs_ = []
        for m in both:
            ms = jnp.sum(cs[m] * hh[m], axis=1, keepdims=True) * (1.0 / width)
            invs_.append(lax.rsqrt(jnp.maximum(ms, 0.0) + EPS))
        fs_ = [mm(cs[m].astype(BF16), ng) for m in both] if s < 15 else []
        old = list(cs)
        for m in both:
            xs[s, m] = (invs_[m] * old[m]).astype(BF16)
            es[s, m] = es_[m]
            hs[s, m] = hh[m]
            invs[s, m] = jnp.broadcast_to(invs_[m], invs.shape[2:])
        if s == 15:
            return None
        ys_ = [mm(mixings[m][0], (invs_[m] * es_[m]).astype(BF16)) for m in both]
        for m in both:
            cs[m] = cs[m] + ys_[m]
        ng = onward(s + 1)
        zs_ = [mm(mixings[m][0], (invs_[m] * fs_[m]).astype(BF16)) for m in both]
        for m in both:
            hh[m] = hh[m] + zs_[m]
        return ng

    start_y(0)
    start_y(1)
    sent(over_y[0])
    start_y(2)
    start_x(0)
    sent(over_y[1])
    start_y(3)
    start_x(1)
    sent(over_y[2])
    start_y(4)
    start_core(0)
    start_x(2)
    start_core(1)
    start_x(3)
    across[0].wait_recv()
    across[1].wait_recv()
    ng = onward(0)
    for s in (0, 1, 2):
        ng = forward(s, ng)
    start_core(2)
    start_x(4)
    start_core(3)
    across[2].wait_recv()
    for s in (3, 4, 5, 6):
        ng = forward(s, ng)
    start_core(4)
    across[3].wait_recv()
    for s in (7, 8, 9, 10):
        ng = forward(s, ng)
    across[4].wait_recv()
    for s in (11, 12, 13, 14, 15):
        ng = forward(s, ng)

    gs = [cot_ref[m].astype(F32) for m in range(micros)]
    for s in reversed(range(16)):
        n = step_of(s)
        both = range(micros)
        ps_ = [mm(mixings[m][1], gs[m].astype(BF16)) for m in both]
        pb_ = [p.astype(BF16) for p in ps_]
        qs_ = [mm(p, n, ((1,), (1,))) for p in pb_] if s > 0 else []
        for m in both:
            ps[s, m] = pb_[m]
            if s > 0:
                inv = invs[s, m][:, :1]
                t = jnp.sum(ps_[m] * es[s, m], axis=1, keepdims=True)
                gs[m] = (gs[m] - (inv * inv * inv * t * (1.0 / width)) * hs[s, m]) + inv * qs_[m]

    rows = micros * xs.shape[2]
    total = mm(xs[at.s].reshape(rows, 256), ps[at.s].reshape(rows, 256), ((0,), (0,)))
    part[...] = total.reshape(16, 16, 256)
    part_b[...] = total.astype(BF16).reshape(16, 16, 256)
    others = far_first(at)
    pieces = [
        send(part_b.at[piece], slots.at[i], rs_send.at[i], rs_recv.at[i], peer)
        for i, (peer, piece) in enumerate(others)
    ]
    mine = part[piece_of(at.d)]
    for i in reversed(range(15)):
        pieces[i].wait_recv()
        mine = mine + slots[i].astype(F32)
    summed = whole.at[piece_of(at.d)]
    summed[...] = mine.astype(BF16)
    spread = [
        send(summed, summed, ag_send.at[i], ag_recv.at[i], peer) for i, (peer, piece) in enumerate(others)
    ]
    sent([swap] + over_z + sum(over_y[3:], []) + sum(over_x, []) + across + pieces)
    for copy in spread:
        copy.wait()


def finish(factor_hbm, folded_hbm, own_gain_hbm, out_hbm, basis_hbm, value_hbm, gv_hbm, go_hbm, gg_hbm,
           factor_ref, folded, own_gain, out, basis, value, gv, go, gg, load_sem, store_sem):
    d = lax.axis_index("dp")
    rows = pl.ds(pl.multiple_of(d * 256, 256), 256)
    loads = [
        pltpu.make_async_copy(factor_hbm, factor_ref, load_sem.at[0]),
        pltpu.make_async_copy(basis_hbm.at[rows, :], basis, load_sem.at[1]),
        pltpu.make_async_copy(out_hbm.at[0], out, load_sem.at[2]),
        pltpu.make_async_copy(own_gain_hbm, own_gain, load_sem.at[3]),
        pltpu.make_async_copy(value_hbm.at[0, rows, :], value, load_sem.at[4]),
        pltpu.make_async_copy(folded_hbm, folded, load_sem.at[5]),
    ]
    for load in loads:
        load.start()
    for load in loads:
        load.wait()
    factor = factor_ref[...].reshape(256, 256)
    left = mm(basis[...], factor).astype(BF16)
    gain = own_gain[:, :1]
    sums = jnp.zeros((256, 1), F32)
    stores = []
    for i in range(4):
        lanes = slice(i * 256, (i + 1) * 256)
        plain = mm(left, out[lanes, :], ((1,), (1,)))
        gv[:, lanes] = gain * plain
        stores.append(pltpu.make_async_copy(
            gv.at[:, lanes], gv_hbm.at[0, :, lanes], store_sem.at[i]))
        stores[-1].start()
        sums = sums + jnp.sum(plain * value[:, lanes].astype(F32), axis=1, keepdims=True)
    go[...] = mm(folded[...], factor, ((0,), (0,)))
    own = pl.ds(pl.multiple_of((d % 2) * 64, 64), 64)
    stores.append(pltpu.make_async_copy(go.at[own, :], go_hbm.at[0], store_sem.at[4]))
    stores[-1].start()
    gg[...] = jnp.broadcast_to(sums, (256, 128)).T[0:1, :]
    stores.append(pltpu.make_async_copy(gg, gg_hbm, store_sem.at[5]))
    stores[-1].start()
    for store in stores:
        store.wait()


def shards(coeffs, cotangent, segment_ids, basis_matrix, section_gains, value_weight, out_weight):
    vmem = pl.BlockSpec(memory_space=pltpu.VMEM)
    hbm = pl.BlockSpec(memory_space=pltpu.HBM)
    dma = pltpu.SemaphoreType.DMA
    shape = jax.ShapeDtypeStruct
    handed = pl.pallas_call(
        relay,
        out_shape=(
            shape((16, 16, 256), BF16),
            shape((256, 128), BF16),
            shape((256, 128), F32),
        ),
        in_specs=[hbm] * 7,
        out_specs=(vmem,) * 3,
        scratch_shapes=[
            pltpu.VMEM((1024, 256), BF16),
            pltpu.VMEM((2048, 1024), BF16),
            pltpu.VMEM((4096, 128), BF16),
            pltpu.VMEM((2048, 256), BF16),
            pltpu.VMEM((4096, 256), BF16),
            pltpu.VMEM((1, 2048), F32),
            pltpu.VMEM((1, 4096), F32),
            pltpu.VMEM((2, 128, 256), BF16),
            pltpu.VMEM((2, 128, 256), BF16),
            pltpu.VMEM((2, 128), jnp.int32),
            pltpu.VMEM((8, 32, 256), F32),
            pltpu.VMEM((8, 32, 256), BF16),
            pltpu.VMEM((32, 256), BF16),
            pltpu.VMEM((128, 256), F32),
            pltpu.VMEM((2, 8, 2, 4, 32, 256), BF16),
            pltpu.VMEM((16, 2, 128, 256), BF16),
            pltpu.VMEM((16, 2, 128, 256), BF16),
            pltpu.VMEM((16, 2, 128, 256), F32),
            pltpu.VMEM((16, 2, 128, 256), F32),
            pltpu.VMEM((16, 2, 128, 128), F32),
            pltpu.VMEM((16, 16, 256), F32),
            pltpu.VMEM((16, 16, 256), BF16),
            pltpu.VMEM((15, 16, 256), BF16),
            dma((12,)), dma, dma, dma((8,)), dma((8,)),
            dma((5, 4)), dma((5, 4)), dma((5, 2)), dma((5, 2)), dma((5,)), dma((5,)),
            dma((15,)), dma((15,)), dma((15,)), dma((15,)),
        ],
        compiler_params=pltpu.CompilerParams(
            collective_id=0, has_side_effects=True, vmem_limit_bytes=VMEM_LIMIT
        ),
    )(basis_matrix, section_gains, value_weight, out_weight, coeffs, cotangent, segment_ids)
    return pl.pallas_call(
        finish,
        out_shape=(
            shape((1, 256, 1024), F32),
            shape((1, 64, 256), F32),
            shape((1, 256), F32),
        ),
        in_specs=[hbm] * 6,
        out_specs=(hbm,) * 3,
        scratch_shapes=[
            pltpu.VMEM((16, 16, 256), BF16),
            pltpu.VMEM((256, 128), BF16),
            pltpu.VMEM((256, 128), F32),
            pltpu.VMEM((1024, 256), BF16),
            pltpu.VMEM((256, 256), BF16),
            pltpu.VMEM((256, 1024), BF16),
            pltpu.VMEM((256, 1024), F32),
            pltpu.VMEM((128, 256), F32),
            pltpu.VMEM((1, 256), F32),
            dma((6,)),
            dma((6,)),
        ],
        compiler_params=pltpu.CompilerParams(vmem_limit_bytes=VMEM_LIMIT),
    )(*handed, out_weight, basis_matrix, value_weight)


def solution(mesh):
    placed = (
        P(None, "dp", None),
        P(None, "dp", None),
        P(None, "dp"),
        P(),
        P("section", None),
        P("section", None, None),
        P("section", None, None),
    )
    return jax.shard_map(
        shards,
        mesh=mesh,
        in_specs=placed,
        out_specs=(P("section", "dp", None), P("section", "dp", None), P("section", "dp")),
        check_vma=False,
    )
```

```python
import jax
import jax.numpy as jnp
from jax import lax
from jax.experimental import pallas as pl
from jax.experimental.pallas import tpu as pltpu
from jax.sharding import PartitionSpec as P

EPS = 1e-05
MESH = pl.DeviceIdType.MESH
F32 = jnp.float32
BF16 = jnp.bfloat16
VMEM_LIMIT = 44 * 1024 * 1024


def mm(a, b, dims=((1,), (0,))):
    return lax.dot_general(a, b, (dims, ((), ())), preferred_element_type=F32)


def mixing_pair(seg_row):
    rows = seg_row.shape[1]
    across = jnp.broadcast_to(seg_row, (rows, rows))
    down = across.T
    i = lax.broadcasted_iota(jnp.int32, (rows, rows), 0)
    j = lax.broadcasted_iota(jnp.int32, (rows, rows), 1)
    same = across == down
    low = jnp.where(same & (j <= i), 1.0, 0.0).astype(F32)
    high = jnp.where(same & (i <= j), 1.0, 0.0).astype(F32)
    mixing = (low / jnp.sum(low, axis=1, keepdims=True)).astype(BF16)
    mixing_t = (high / jnp.sum(high, axis=0, keepdims=True)).astype(BF16)
    return mixing, mixing_t


class Place:
    def __init__(self):
        self.s = lax.axis_index("section")
        self.d = lax.axis_index("dp")
        self.z = self.s // 2
        self.xl = self.s % 2
        self.y = self.d // 4
        self.xh = (self.d // 2) % 2
        self.core = self.d % 2
        self.x = self.xh * 2 + self.xl

    def dp_peer(self, k):
        return (self.s, (self.d + k) % 16)

    def z_peer(self, k):
        return (((self.z + k) % 8) * 2 + self.xl, self.d)

    def y_peer(self, k):
        return (self.s, ((self.y + k) % 4) * 4 + self.xh * 2 + self.core)

    def x_peer(self, k):
        x = (self.x + k) % 4
        return (self.z * 2 + x % 2, self.y * 4 + (x // 2) * 2 + self.core)

    def core_peer(self):
        return (self.s, self.y * 4 + self.xh * 2 + (self.core + 1) % 2)


def piece_of(d):
    return (d % 2) * 8 + d // 2


def send(src, dst, send_sem, recv_sem, peer):
    copy = pltpu.make_async_remote_copy(
        src_ref=src, dst_ref=dst, send_sem=send_sem, recv_sem=recv_sem,
        device_id=peer, device_id_type=MESH,
    )
    copy.start()
    return copy


def far_first(at):
    hops = lambda o: min(o[0], 4 - o[0]) + 2 * o[1]
    offsets = [(y, xh, c) for y in range(4) for xh in range(2) for c in range(2) if (y, xh, c) != (0, 0, 0)]
    offsets.sort(key=lambda o: -hops(o))
    peers = []
    for y, xh, c in offsets:
        y_to, xh_to, c_to = (at.y + y) % 4, (at.xh + xh) % 2, (at.core + c) % 2
        peers.append(((at.s, y_to * 4 + xh_to * 2 + c_to), c_to * 8 + y_to * 2 + xh_to))
    return peers


def relay(
    basis_hbm, gain_hbm, value_hbm, out_hbm, c_hbm, cot_hbm, seg_hbm,
    whole, out, basis_own, value_own, folded_ref, own_gain_ref,
    value, value_cols, basis_half, basis, gain_half, gain, c_ref, cot_ref, seg_ref,
    part_n, part_nb, slot_n, gain_pad, every, xs, ps, es, hs, invs, part, part_b, slots,
    load_sem, n_send, n_recv, z_send, z_recv, y_send, y_recv, x_send, x_recv, c_send, c_recv,
    rs_send, rs_recv, ag_send, ag_recv,
):
    at = Place()
    width = basis.shape[0]
    half = width // 2
    cuts = (0, 512, 1024, 1536, 2048)
    start = pl.multiple_of(at.core * half, half)

    def load(i, src, dst):
        copy = pltpu.make_async_copy(src, dst, load_sem.at[i])
        copy.start()
        return copy

    early = [
        load(0, gain_hbm.at[:, pl.ds(start, half)], gain_half),
        load(1, basis_hbm.at[pl.ds(start, half), :], basis_half),
        load(2, out_hbm.at[0], out),
    ]
    for i in range(len(cuts) - 1):
        size = cuts[i + 1] - cuts[i]
        rows = pl.ds(pl.multiple_of(start + cuts[i], 512), size)
        early.append(load(3 + i, value_hbm.at[0, rows, :], value.at[pl.ds(cuts[i], size), :]))
    barrier = pltpu.get_barrier_semaphore()
    peers = [at.z_peer(k) for k in (4, 3, 5, 2, 6, 1, 7)] + [at.dp_peer(k) for k in range(1, 16)]
    peers += [at.x_peer(1), at.x_peer(3)]
    for peer in peers:
        pl.semaphore_signal(barrier, inc=1, device_id=peer, device_id_type=MESH)
    own_rows = pl.ds(pl.multiple_of(at.d * 256, 256), 256)
    cols = pl.ds(pl.multiple_of((at.d // 2) * 128, 128), 128)
    late = [
        load(7, basis_hbm, basis),
        load(8, value_hbm.at[0, :, cols], value_cols),
        load(9, gain_hbm, gain),
        load(10, c_hbm, c_ref),
        load(11, seg_hbm, seg_ref),
        load(12, cot_hbm, cot_ref),
        load(13, basis_hbm.at[own_rows, :], basis_own),
        load(14, value_hbm.at[0, own_rows, :], value_own),
    ]

    partial = jnp.zeros((256, 256), F32)
    for copy in early[:3]:
        copy.wait()
    before = None
    for i in range(len(cuts) - 1):
        lanes = slice(cuts[i], cuts[i + 1])
        scaled = (basis_half[lanes, :].astype(F32).T * gain_half[0:1, lanes]).astype(BF16)
        early[3 + i].wait()
        through = mm(value[lanes, :], out[...]).astype(BF16)
        if before is not None:
            partial = partial + mm(*before)
        before = (scaled, through)
    partial = partial + mm(*before)
    part_n[...] = partial.reshape(8, 32, 256)
    part_nb[...] = partial.astype(BF16).reshape(8, 32, 256)

    pl.semaphore_wait(barrier, len(peers))
    other = (at.core + 1) % 2
    swap = send(part_nb.at[other * 4 + at.y], slot_n, n_send, n_recv, at.core_peer())
    swap.wait_recv()
    own = every.at[at.core, at.z, at.xl, at.y]
    own[...] = (part_n[at.core * 4 + at.y] + slot_n[...].astype(F32)).astype(BF16)
    over_z = [send(own, own, z_send.at[k], z_recv.at[at.z], at.z_peer(k)) for k in (4, 3, 5, 2, 6, 1, 7)]

    for copy in late:
        copy.wait()
    gram = jnp.zeros((256, 256), F32)
    folded = jnp.zeros((256, 128), F32)
    for i in range(8):
        lanes = slice(i * 512, (i + 1) * 512)
        chunk = basis[lanes, :]
        chunk_t = chunk.astype(F32).T
        gram = gram + mm(chunk_t.astype(BF16), chunk)
        scaled = (chunk_t * gain[0:1, lanes]).astype(BF16)
        folded = folded + mm(scaled, value_cols[lanes, :])
    folded_ref[...] = folded.astype(BF16)
    gram_b = gram.astype(BF16)
    for i in range(16):
        gain_pad[i : i + 1, :] = gain[0:1, i * 256 : (i + 1) * 256]
    gain_pad[16:128, :] = jnp.zeros((112, 256), F32)
    gain_cols = gain_pad[...].T
    lane = lax.broadcasted_iota(jnp.int32, gain_cols.shape, 1)
    own_gain = jnp.sum(jnp.where(lane == at.d, gain_cols, 0.0), axis=1, keepdims=True)
    own_gain_ref[...] = jnp.broadcast_to(own_gain, own_gain_ref.shape)
    micros = c_ref.shape[0]
    mixings = [mixing_pair(seg_ref[m : m + 1, :].astype(F32)) for m in range(micros)]
    cs = [c_ref[m].astype(F32) for m in range(micros)]
    hh = [mm(c_ref[m], gram_b) for m in range(micros)]

    bounds = (0, 1, 2, 4, 6, 7, 8)
    over_y, over_x, across = [], [], []

    def arrived(z):
        @pl.when(at.z != z)
        def _():
            there = every.at[at.core, z, at.xl, at.y]
            pltpu.make_async_remote_copy(
                src_ref=there, dst_ref=there, send_sem=z_send.at[0], recv_sem=z_recv.at[z],
                device_id=at.core_peer(), device_id_type=MESH,
            ).wait_recv()

    def planes(q):
        return pl.ds(bounds[q], bounds[q + 1] - bounds[q])

    def start_y(q):
        for z in range(bounds[q], bounds[q + 1]):
            arrived(z)
        mine = every.at[at.core, planes(q), at.xl, at.y]
        over_y.append(
            [send(mine, mine, y_send.at[q, k], y_recv.at[q, k], at.y_peer(k)) for k in (2, 1, 3)]
        )

    def start_x(q):
        for copy in over_y[q]:
            copy.wait_recv()
        low = every.at[at.core, planes(q), at.xl, pl.ds(0, 2)]
        high = every.at[at.core, planes(q), at.xl, pl.ds(2, 2)]
        over_x.append([
            send(low, low, x_send.at[q, 0], x_recv.at[q, 0], at.x_peer(1)),
            send(high, high, x_send.at[q, 1], x_recv.at[q, 1], at.x_peer(3)),
        ])

    def start_core(q):
        for copy in over_x[q]:
            copy.wait_recv()
        chunk = every.at[at.core, planes(q)]
        across.append(send(chunk, chunk, c_send.at[q], c_recv.at[q], at.core_peer()))

    def sent(copies):
        for copy in copies:
            copy.wait_send()

    def step_of(s):
        z, xl = s // 2, s % 2
        return every[:, z, xl].reshape(256, 256)

    def onward(s):
        return mm(step_of(s), gram_b).astype(BF16)

    def forward(s, ng):
        n = step_of(s)
        both = range(micros)
        es_ = [mm(cs[m].astype(BF16), n) for m in both]
        invs_ = []
        for m in both:
            ms = jnp.sum(cs[m] * hh[m], axis=1, keepdims=True) * (1.0 / width)
            invs_.append(lax.rsqrt(jnp.maximum(ms, 0.0) + EPS))
        fs_ = [mm(cs[m].astype(BF16), ng) for m in both] if s < 15 else []
        old = list(cs)
        for m in both:
            xs[s, m] = (invs_[m] * old[m]).astype(BF16)
            es[s, m] = es_[m]
            hs[s, m] = hh[m]
            invs[s, m] = jnp.broadcast_to(invs_[m], invs.shape[2:])
        if s == 15:
            return None
        ys_ = [mm(mixings[m][0], (invs_[m] * es_[m]).astype(BF16)) for m in both]
        for m in both:
            cs[m] = cs[m] + ys_[m]
        ng = onward(s + 1)
        zs_ = [mm(mixings[m][0], (invs_[m] * fs_[m]).astype(BF16)) for m in both]
        for m in both:
            hh[m] = hh[m] + zs_[m]
        return ng

    start_y(0)
    start_y(1)
    sent(over_y[0])
    start_y(2)
    start_x(0)
    sent(over_y[1])
    start_y(3)
    start_x(1)
    sent(over_y[2])
    start_y(4)
    start_core(0)
    start_x(2)
    start_y(5)
    start_core(1)
    start_x(3)
    across[0].wait_recv()
    across[1].wait_recv()
    ng = onward(0)
    for s in (0, 1, 2):
        ng = forward(s, ng)
    start_core(2)
    start_x(4)
    start_x(5)
    start_core(3)
    across[2].wait_recv()
    for s in (3, 4, 5, 6):
        ng = forward(s, ng)
    start_core(4)
    across[3].wait_recv()
    for s in (7, 8, 9):
        ng = forward(s, ng)
    start_core(5)
    for s in (10,):
        ng = forward(s, ng)
    across[4].wait_recv()
    for s in (11, 12):
        ng = forward(s, ng)
    across[5].wait_recv()
    for s in (13, 14, 15):
        ng = forward(s, ng)

    gs = [cot_ref[m].astype(F32) for m in range(micros)]
    for s in reversed(range(16)):
        n = step_of(s)
        both = range(micros)
        ps_ = [mm(mixings[m][1], gs[m].astype(BF16)) for m in both]
        pb_ = [p.astype(BF16) for p in ps_]
        qs_ = [mm(p, n, ((1,), (1,))) for p in pb_] if s > 0 else []
        for m in both:
            ps[s, m] = pb_[m]
            if s > 0:
                inv = invs[s, m][:, :1]
                t = jnp.sum(ps_[m] * es[s, m], axis=1, keepdims=True)
                gs[m] = (gs[m] - (inv * inv * inv * t * (1.0 / width)) * hs[s, m]) + inv * qs_[m]

    rows = micros * xs.shape[2]
    total = mm(xs[at.s].reshape(rows, 256), ps[at.s].reshape(rows, 256), ((0,), (0,)))
    part[...] = total.reshape(16, 16, 256)
    part_b[...] = total.astype(BF16).reshape(16, 16, 256)
    others = far_first(at)
    pieces = [
        send(part_b.at[piece], slots.at[i], rs_send.at[i], rs_recv.at[i], peer)
        for i, (peer, piece) in enumerate(others)
    ]
    mine = part[piece_of(at.d)]
    for i in reversed(range(15)):
        pieces[i].wait_recv()
        mine = mine + slots[i].astype(F32)
    summed = whole.at[piece_of(at.d)]
    summed[...] = mine.astype(BF16)
    spread = [
        send(summed, summed, ag_send.at[i], ag_recv.at[i], peer) for i, (peer, piece) in enumerate(others)
    ]
    sent([swap] + over_z + sum(over_y[3:], []) + sum(over_x, []) + across + pieces)
    for copy in spread:
        copy.wait()


def finish(factor_ref, out, basis, value, folded, own_gain, gv_hbm, go_hbm, gg_hbm,
           gv, go, gg, store_sem):
    d = lax.axis_index("dp")
    factor = factor_ref[...].reshape(256, 256)
    left = mm(basis[...], factor).astype(BF16)
    gain = own_gain[:, :1]
    sums = jnp.zeros((256, 1), F32)
    stores = []
    for i in range(4):
        lanes = slice(i * 256, (i + 1) * 256)
        plain = mm(left, out[lanes, :], ((1,), (1,)))
        gv[:, lanes] = gain * plain
        stores.append(pltpu.make_async_copy(
            gv.at[:, lanes], gv_hbm.at[0, :, lanes], store_sem.at[i]))
        stores[-1].start()
        sums = sums + jnp.sum(plain * value[:, lanes].astype(F32), axis=1, keepdims=True)
    go[...] = mm(folded[...], factor, ((0,), (0,)))
    own = pl.ds(pl.multiple_of((d % 2) * 64, 64), 64)
    stores.append(pltpu.make_async_copy(go.at[own, :], go_hbm.at[0], store_sem.at[4]))
    stores[-1].start()
    gg[...] = jnp.broadcast_to(sums, (256, 128)).T[0:1, :]
    stores.append(pltpu.make_async_copy(gg, gg_hbm, store_sem.at[5]))
    stores[-1].start()
    for store in stores:
        store.wait()


def shards(coeffs, cotangent, segment_ids, basis_matrix, section_gains, value_weight, out_weight):
    vmem = pl.BlockSpec(memory_space=pltpu.VMEM)
    hbm = pl.BlockSpec(memory_space=pltpu.HBM)
    dma = pltpu.SemaphoreType.DMA
    shape = jax.ShapeDtypeStruct
    operands = (basis_matrix, section_gains, value_weight, out_weight, coeffs, cotangent, segment_ids)
    operands = [pltpu.with_memory_space_constraint(x, pltpu.HBM) for x in operands]
    handed = pl.pallas_call(
        relay,
        out_shape=(
            shape((16, 16, 256), BF16),
            shape((1024, 256), BF16),
            shape((256, 256), BF16),
            shape((256, 1024), BF16),
            shape((256, 128), BF16),
            shape((256, 128), F32),
        ),
        in_specs=[hbm] * 7,
        out_specs=(vmem,) * 6,
        scratch_shapes=[
            pltpu.VMEM((2048, 1024), BF16),
            pltpu.VMEM((4096, 128), BF16),
            pltpu.VMEM((2048, 256), BF16),
            pltpu.VMEM((4096, 256), BF16),
            pltpu.VMEM((1, 2048), F32),
            pltpu.VMEM((1, 4096), F32),
            pltpu.VMEM((2, 128, 256), BF16),
            pltpu.VMEM((2, 128, 256), BF16),
            pltpu.VMEM((2, 128), jnp.int32),
            pltpu.VMEM((8, 32, 256), F32),
            pltpu.VMEM((8, 32, 256), BF16),
            pltpu.VMEM((32, 256), BF16),
            pltpu.VMEM((128, 256), F32),
            pltpu.VMEM((2, 8, 2, 4, 32, 256), BF16),
            pltpu.VMEM((16, 2, 128, 256), BF16),
            pltpu.VMEM((16, 2, 128, 256), BF16),
            pltpu.VMEM((16, 2, 128, 256), F32),
            pltpu.VMEM((16, 2, 128, 256), F32),
            pltpu.VMEM((16, 2, 128, 128), F32),
            pltpu.VMEM((16, 16, 256), F32),
            pltpu.VMEM((16, 16, 256), BF16),
            pltpu.VMEM((15, 16, 256), BF16),
            dma((15,)), dma, dma, dma((8,)), dma((8,)),
            dma((6, 4)), dma((6, 4)), dma((6, 2)), dma((6, 2)), dma((6,)), dma((6,)),
            dma((15,)), dma((15,)), dma((15,)), dma((15,)),
        ],
        compiler_params=pltpu.CompilerParams(
            collective_id=0, has_side_effects=True, vmem_limit_bytes=VMEM_LIMIT
        ),
    )(*operands)
    return pl.pallas_call(
        finish,
        out_shape=(
            shape((1, 256, 1024), F32),
            shape((1, 64, 256), F32),
            shape((1, 256), F32),
        ),
        in_specs=[vmem] * 6,
        out_specs=(hbm,) * 3,
        scratch_shapes=[
            pltpu.VMEM((256, 1024), F32),
            pltpu.VMEM((128, 256), F32),
            pltpu.VMEM((1, 256), F32),
            dma((6,)),
        ],
        compiler_params=pltpu.CompilerParams(vmem_limit_bytes=16 * 1024 * 1024),
    )(*handed)


def solution(mesh):
    placed = (
        P(None, "dp", None),
        P(None, "dp", None),
        P(None, "dp"),
        P(),
        P("section", None),
        P("section", None, None),
        P("section", None, None),
    )
    return jax.shard_map(
        shards,
        mesh=mesh,
        in_specs=placed,
        out_specs=(P("section", "dp", None), P("section", "dp", None), P("section", "dp")),
        check_vma=False,
    )
```

```python
import jax
import jax.numpy as jnp
from jax import lax
from jax.experimental import pallas as pl
from jax.experimental.pallas import tpu as pltpu
from jax.sharding import PartitionSpec as P

EPS = 1e-05
MESH = pl.DeviceIdType.MESH
F32 = jnp.float32
BF16 = jnp.bfloat16
VMEM_LIMIT = 44 * 1024 * 1024


def mm(a, b, dims=((1,), (0,))):
    return lax.dot_general(a, b, (dims, ((), ())), preferred_element_type=F32)


def mixing_pair(seg_row):
    rows = seg_row.shape[1]
    across = jnp.broadcast_to(seg_row, (rows, rows))
    down = across.T
    i = lax.broadcasted_iota(jnp.int32, (rows, rows), 0)
    j = lax.broadcasted_iota(jnp.int32, (rows, rows), 1)
    same = across == down
    low = jnp.where(same & (j <= i), 1.0, 0.0).astype(F32)
    high = jnp.where(same & (i <= j), 1.0, 0.0).astype(F32)
    mixing = (low / jnp.sum(low, axis=1, keepdims=True)).astype(BF16)
    mixing_t = (high / jnp.sum(high, axis=0, keepdims=True)).astype(BF16)
    return mixing, mixing_t


class Place:
    def __init__(self):
        self.s = lax.axis_index("section")
        self.d = lax.axis_index("dp")
        self.z = lax.div(self.s, 2)
        self.xl = lax.rem(self.s, 2)
        self.y = lax.div(self.d, 4)
        self.xh = lax.rem(lax.div(self.d, 2), 2)
        self.core = lax.rem(self.d, 2)
        x = self.xh * 2 + self.xl
        self.ys = [lax.rem(self.y + k, 4) for k in range(4)]
        self.xhs = [self.xh] + [lax.div(lax.rem(x + k, 4), 2) for k in range(1, 4)]
        self.twin = self.s + 1 - 2 * self.xl
        self.rows = [y * 4 for y in self.ys]

    def z_peer(self, k):
        return (lax.rem(self.z + k, 8) * 2 + self.xl, self.d)

    def member(self, dx, dy, core):
        section = self.s if dx % 2 == 0 else self.twin
        return (section, self.rows[dy] + self.xhs[dx] * 2 + core)

    def y_peer(self, k):
        return self.member(0, k, self.core)

    def x_peer(self, k):
        return self.member(k, 0, self.core)

    def core_peer(self):
        return self.member(0, 0, 1 - self.core)


def remote(src, dst, send_sem, recv_sem, peer):
    return pltpu.make_async_remote_copy(
        src_ref=src, dst_ref=dst, send_sem=send_sem, recv_sem=recv_sem,
        device_id=peer, device_id_type=MESH,
    )


def send(src, dst, send_sem, recv_sem, peer):
    copy = remote(src, dst, send_sem, recv_sem, peer)
    copy.start()
    return copy


def relay(
    basis_hbm, gain_hbm, value_hbm, out_hbm, c_hbm, cot_hbm, seg_hbm,
    whole, out, basis_own, value_own, folded_ref, own_gain_ref,
    value, value_cols, basis_half, basis, gain_half, gain, c_ref, cot_ref, seg_ref,
    part_n, part_nb, slot_n, gain_pad, every, xs, grads, es, hs, invs, left_t, part, part_b, slots, summed,
    load_sem, n_send, n_recv, z_send, z_recv, y_send, y_recv, x_send, x_recv, c_send, c_recv,
    rs_send, rs_recv, ag_send, ag_recv,
):
    at = Place()
    width = basis.shape[0]
    half = width // 2
    cuts = (0, 256, 768, 1280, 1792, 2048)
    start = pl.multiple_of(at.core * half, half)

    def load(i, src, dst):
        copy = pltpu.make_async_copy(src, dst, load_sem.at[i])
        copy.start()
        return copy

    gain_half_load = load(0, gain_hbm.at[:, pl.ds(start, half)], gain_half)
    early = []
    for i in range(len(cuts) - 1):
        size = cuts[i + 1] - cuts[i]
        rows, here = pl.ds(pl.multiple_of(start + cuts[i], 256), size), pl.ds(cuts[i], size)
        early.append((
            load(1 + 2 * i, basis_hbm.at[rows, :], basis_half.at[here, :]),
            load(2 + 2 * i, value_hbm.at[0, rows, :], value.at[here, :]),
        ))
    out_load = load(11, out_hbm.at[0], out)
    barrier = pltpu.get_barrier_semaphore()
    peers = [at.z_peer(k) for k in (4, 3, 5, 2, 6, 1, 7)]
    peers += [at.member(dx, dy, core) for dx in (1, 3) for dy in (2, 1, 3, 0) for core in (0, 1)]
    peers += [at.member(0, dy, core) for dy in (2, 1, 3) for core in (0, 1)] + [at.core_peer()]
    for peer in peers:
        pl.semaphore_signal(barrier, inc=1, device_id=peer, device_id_type=MESH)
    own_rows = pl.ds(pl.multiple_of(at.d * 256, 256), 256)
    cols = pl.ds(pl.multiple_of(lax.div(at.d, 2) * 128, 128), 128)
    late = [
        load(12, basis_hbm, basis),
        load(13, value_hbm.at[0, :, cols], value_cols),
        load(14, gain_hbm, gain),
        load(15, c_hbm, c_ref),
        load(16, seg_hbm, seg_ref),
        load(17, cot_hbm, cot_ref),
        load(18, basis_hbm.at[own_rows, :], basis_own),
        load(19, value_hbm.at[0, own_rows, :], value_own),
    ]

    gain_half_load.wait()
    wide = jnp.zeros((256, out.shape[0]), F32)
    for i in range(len(cuts) - 1):
        lanes = slice(cuts[i], cuts[i + 1])
        early[i][0].wait()
        scaled = (basis_half[lanes, :].astype(F32).T * gain_half[0:1, lanes]).astype(BF16)
        early[i][1].wait()
        wide = wide + mm(scaled, value[lanes, :])
    out_load.wait()
    partial = mm(wide.astype(BF16), out[...])
    part_n[...] = partial.reshape(8, 32, 256)
    part_nb[...] = partial.astype(BF16).reshape(8, 32, 256)

    pl.semaphore_wait(barrier, len(peers))
    other = 1 - at.core
    swap = send(part_nb.at[other * 4 + at.y], slot_n, n_send, n_recv, at.core_peer())
    swap.wait_recv()
    own = every.at[at.core, at.z, at.xl, at.y]
    own[...] = (part_n[at.core * 4 + at.y] + slot_n[...].astype(F32)).astype(BF16)
    over_z = [send(own, own, z_send.at[k], z_recv.at[at.z], at.z_peer(k)) for k in (4, 3, 5, 2, 6, 1, 7)]

    for copy in late:
        copy.wait()
    gram = jnp.zeros((256, 256), F32)
    folded = jnp.zeros((256, 128), F32)
    for i in range(8):
        lanes = slice(i * 512, (i + 1) * 512)
        chunk = basis[lanes, :]
        chunk_t = chunk.astype(F32).T
        gram = gram + mm(chunk_t.astype(BF16), chunk)
        scaled = (chunk_t * gain[0:1, lanes]).astype(BF16)
        folded = folded + mm(scaled, value_cols[lanes, :])
    folded_ref[...] = folded.astype(BF16)
    gram_b = gram.astype(BF16)
    for i in range(16):
        gain_pad[i : i + 1, :] = gain[0:1, i * 256 : (i + 1) * 256]
    gain_pad[16:128, :] = jnp.zeros((112, 256), F32)
    gain_cols = gain_pad[...].T
    lane = lax.broadcasted_iota(jnp.int32, gain_cols.shape, 1)
    own_gain = jnp.sum(jnp.where(lane == at.d, gain_cols, 0.0), axis=1, keepdims=True)
    own_gain_ref[...] = jnp.broadcast_to(own_gain, own_gain_ref.shape)
    micros = c_ref.shape[0]
    mixings = [mixing_pair(seg_ref[m : m + 1, :].astype(F32)) for m in range(micros)]
    cs = [c_ref[m].astype(F32) for m in range(micros)]
    hh = [mm(c_ref[m], gram_b) for m in range(micros)]

    bounds = (0, 2, 4, 6, 8)
    over_y, over_x, across = [], [], []

    def arrived(z):
        @pl.when(at.z != z)
        def _():
            there = every.at[at.core, z, at.xl, at.y]
            remote(there, there, z_send.at[0], z_recv.at[z], at.core_peer()).wait_recv()

    def planes(q):
        return pl.ds(bounds[q], bounds[q + 1] - bounds[q])

    def start_y(q):
        for z in range(bounds[q], bounds[q + 1]):
            arrived(z)
        mine = every.at[at.core, planes(q), at.xl, at.y]
        over_y.append(
            [send(mine, mine, y_send.at[q, k], y_recv.at[q, k], at.y_peer(k)) for k in (2, 1, 3)]
        )

    def start_x(q):
        for copy in over_y[q]:
            copy.wait_recv()
        low = every.at[at.core, planes(q), at.xl, pl.ds(0, 2)]
        high = every.at[at.core, planes(q), at.xl, pl.ds(2, 2)]
        over_x.append([
            send(low, low, x_send.at[q, 0], x_recv.at[q, 0], at.x_peer(1)),
            send(high, high, x_send.at[q, 1], x_recv.at[q, 1], at.x_peer(3)),
        ])

    def start_core(q):
        for copy in over_x[q]:
            copy.wait_recv()
        chunk = every.at[at.core, planes(q)]
        across.append(send(chunk, chunk, c_send.at[q], c_recv.at[q], at.core_peer()))

    def sent(copies):
        for copy in copies:
            copy.wait_send()

    def step_of(s):
        z, xl = s // 2, s % 2
        return every[:, z, xl].reshape(256, 256)

    def onward(s):
        return mm(step_of(s), gram_b).astype(BF16)

    def forward(s, ng):
        n = step_of(s)
        both = range(micros)
        es_ = [mm(cs[m].astype(BF16), n) for m in both]
        invs_ = []
        for m in both:
            ms = jnp.sum(cs[m] * hh[m], axis=1, keepdims=True) * (1.0 / width)
            invs_.append(lax.rsqrt(jnp.maximum(ms, 0.0) + EPS))
        fs_ = [mm(cs[m].astype(BF16), ng) for m in both] if s < 15 else []
        old = list(cs)
        for m in both:
            xs[s, m] = (invs_[m] * old[m]).astype(BF16)
            es[s, m] = es_[m]
            hs[s, m] = hh[m]
            invs[s, m] = jnp.broadcast_to(invs_[m], invs.shape[2:])
        if s == 15:
            return None
        ys_ = [mm(mixings[m][0], (invs_[m] * es_[m]).astype(BF16)) for m in both]
        for m in both:
            cs[m] = cs[m] + ys_[m]
        ng = onward(s + 1)
        zs_ = [mm(mixings[m][0], (invs_[m] * fs_[m]).astype(BF16)) for m in both]
        for m in both:
            hh[m] = hh[m] + zs_[m]
        return ng

    start_y(0)
    start_y(1)
    sent(over_y[0])
    start_y(2)
    start_x(0)
    sent(over_y[1])
    start_y(3)
    start_x(1)
    start_core(0)
    start_x(2)
    start_core(1)
    start_x(3)
    across[0].wait_recv()
    ng = onward(0)
    for s in (0, 1, 2):
        ng = forward(s, ng)
    across[1].wait_recv()
    start_core(2)
    for s in (3, 4, 5, 6):
        ng = forward(s, ng)
    start_core(3)
    across[2].wait_recv()
    for s in (7, 8, 9, 10):
        ng = forward(s, ng)
    across[3].wait_recv()
    for s in (11, 12, 13, 14, 15):
        ng = forward(s, ng)

    twin = at.twin
    lanes_here = pl.ds(pl.multiple_of(at.xh * 128, 128), 128)
    lanes_over = pl.ds(pl.multiple_of((1 - at.xh) * 128, 128), 128)

    def left_factor(i, s, lanes):
        for m in range(micros):
            mixed = mm(mixings[m][0], xs[s, m, :, lanes])
            left_t[i, :, m * 128 : (m + 1) * 128] = mixed.T.astype(BF16)

    gs = [cot_ref[m].astype(F32) for m in range(micros)]
    both = range(micros)
    for s in reversed(range(16)):
        for m in both:
            grads[s, m] = gs[m].astype(BF16)
        if s == 0:
            break
        n = step_of(s)
        ps_ = [mm(mixings[m][1], gs[m].astype(BF16)) for m in both]
        qs_ = [mm(p.astype(BF16), n, ((1,), (1,))) for p in ps_]
        for m in both:
            inv = invs[s, m][:, :1]
            t = jnp.sum(ps_[m] * es[s, m], axis=1, keepdims=True)
            gs[m] = (gs[m] - (inv * inv * inv * t * (1.0 / width)) * hs[s, m]) + inv * qs_[m]
        if s == 15:
            left_factor(0, twin, lanes_here)
        if s == 14:
            left_factor(1, at.s, lanes_over)

    rows = micros * 128
    over = mm(left_t[1], grads[at.s].reshape(rows, 256))
    part_b[1] = over.astype(BF16).reshape(4, 32, 256)
    pieces = []
    for i, dy in enumerate((2, 1, 3, 0)):
        j = 2 * i + at.core
        pieces.append(send(
            part_b.at[1, at.ys[dy]], slots.at[j], rs_send.at[i], rs_recv.at[j],
            (at.twin, at.rows[dy] + (1 - at.xh) * 2 + 1)))
    here = mm(left_t[0], grads[twin].reshape(rows, 256))
    part[...] = here.reshape(4, 32, 256)
    part_b[0] = here.astype(BF16).reshape(4, 32, 256)
    for i, dy in enumerate((2, 1, 3)):
        j = 8 + 2 * i + at.core
        pieces.append(send(
            part_b.at[0, at.ys[dy]], slots.at[j], rs_send.at[4 + i], rs_recv.at[j],
            at.member(0, dy, 1)))
    beside = remote(part_b.at[0, at.y], slots.at[14], rs_send.at[7], rs_recv.at[14], at.core_peer())
    place = whole.at[at.xh, at.y]
    spread = [
        remote(summed, place, ag_send.at[i, j], ag_recv.at[i, j], at.member(dx, dy, at.core))
        for i, dy in enumerate((2, 1, 3, 0)) for j, dx in enumerate((1, 3))
    ]
    hand = remote(summed, summed, rs_send.at[8], rs_recv.at[15], at.core_peer())

    @pl.when(at.core == 0)
    def _():
        beside.start()
        hand.wait_recv()

    @pl.when(at.core == 1)
    def _():
        mine = part[at.y]
        for j in (14, 12, 13, 10, 11, 8, 9, 6, 7, 4, 5, 2, 3, 0, 1):
            remote(slots.at[j], slots.at[j], rs_send.at[0], rs_recv.at[j], at.core_peer()).wait_recv()
            mine = mine + slots[j].astype(F32)
        summed[...] = mine.astype(BF16)
        hand.start()

    for copy in spread:
        copy.start()
    sent([swap] + over_z + sum(over_y[2:], []) + sum(over_x, []) + across + pieces)
    sent(spread)

    @pl.when(at.core == 0)
    def _():
        beside.wait_send()

    @pl.when(at.core == 1)
    def _():
        hand.wait_send()

    for i, dy in enumerate((2, 1, 3, 0)):
        for j, dx in enumerate((1, 3)):
            there = whole.at[at.xhs[4 - dx], at.ys[(4 - dy) % 4]]
            remote(there, there, ag_send.at[0, 0], ag_recv.at[i, j], at.core_peer()).wait_recv()


def finish(factor_ref, out, basis, value, folded, own_gain, gv_hbm, go_hbm, gg_hbm,
           gv, go, gg, store_sem):
    d = lax.axis_index("dp")
    factor = factor_ref[...].reshape(256, 256)
    left = mm(basis[...], factor).astype(BF16)
    gain = own_gain[:, :1]
    sums = jnp.zeros((256, 1), F32)
    stores = []
    for i in range(4):
        lanes = slice(i * 256, (i + 1) * 256)
        plain = mm(left, out[lanes, :], ((1,), (1,)))
        gv[:, lanes] = gain * plain
        stores.append(pltpu.make_async_copy(
            gv.at[:, lanes], gv_hbm.at[0, :, lanes], store_sem.at[i]))
        stores[-1].start()
        sums = sums + jnp.sum(plain * value[:, lanes].astype(F32), axis=1, keepdims=True)
    go[...] = mm(folded[...], factor, ((0,), (0,)))
    own = pl.ds(pl.multiple_of((d % 2) * 64, 64), 64)
    stores.append(pltpu.make_async_copy(go.at[own, :], go_hbm.at[0], store_sem.at[4]))
    stores[-1].start()
    gg[...] = jnp.broadcast_to(sums, (256, 128)).T[0:1, :]
    stores.append(pltpu.make_async_copy(gg, gg_hbm, store_sem.at[5]))
    stores[-1].start()
    for store in stores:
        store.wait()


def shards(coeffs, cotangent, segment_ids, basis_matrix, section_gains, value_weight, out_weight):
    vmem = pl.BlockSpec(memory_space=pltpu.VMEM)
    hbm = pl.BlockSpec(memory_space=pltpu.HBM)
    dma = pltpu.SemaphoreType.DMA
    shape = jax.ShapeDtypeStruct
    operands = (basis_matrix, section_gains, value_weight, out_weight, coeffs, cotangent, segment_ids)
    operands = [pltpu.with_memory_space_constraint(x, pltpu.HBM) for x in operands]
    handed = pl.pallas_call(
        relay,
        out_shape=(
            shape((2, 4, 32, 256), BF16),
            shape((1024, 256), BF16),
            shape((256, 256), BF16),
            shape((256, 1024), BF16),
            shape((256, 128), BF16),
            shape((256, 128), F32),
        ),
        in_specs=[hbm] * 7,
        out_specs=(vmem,) * 6,
        scratch_shapes=[
            pltpu.VMEM((2048, 1024), BF16),
            pltpu.VMEM((4096, 128), BF16),
            pltpu.VMEM((2048, 256), BF16),
            pltpu.VMEM((4096, 256), BF16),
            pltpu.VMEM((1, 2048), F32),
            pltpu.VMEM((1, 4096), F32),
            pltpu.VMEM((2, 128, 256), BF16),
            pltpu.VMEM((2, 128, 256), BF16),
            pltpu.VMEM((2, 128), jnp.int32),
            pltpu.VMEM((8, 32, 256), F32),
            pltpu.VMEM((8, 32, 256), BF16),
            pltpu.VMEM((32, 256), BF16),
            pltpu.VMEM((128, 256), F32),
            pltpu.VMEM((2, 8, 2, 4, 32, 256), BF16),
            pltpu.VMEM((16, 2, 128, 256), BF16),
            pltpu.VMEM((16, 2, 128, 256), BF16),
            pltpu.VMEM((16, 2, 128, 256), F32),
            pltpu.VMEM((16, 2, 128, 256), F32),
            pltpu.VMEM((16, 2, 128, 128), F32),
            pltpu.VMEM((2, 128, 256), BF16),
            pltpu.VMEM((4, 32, 256), F32),
            pltpu.VMEM((2, 4, 32, 256), BF16),
            pltpu.VMEM((15, 32, 256), BF16),
            pltpu.VMEM((32, 256), BF16),
            dma((20,)), dma, dma, dma((8,)), dma((8,)),
            dma((4, 4)), dma((4, 4)), dma((4, 2)), dma((4, 2)), dma((4,)), dma((4,)),
            dma((9,)), dma((16,)), dma((4, 2)), dma((4, 2)),
        ],
        compiler_params=pltpu.CompilerParams(
            collective_id=0, has_side_effects=True, vmem_limit_bytes=VMEM_LIMIT
        ),
    )(*operands)
    return pl.pallas_call(
        finish,
        out_shape=(
            shape((1, 256, 1024), F32),
            shape((1, 64, 256), F32),
            shape((1, 256), F32),
        ),
        in_specs=[vmem] * 6,
        out_specs=(hbm,) * 3,
        scratch_shapes=[
            pltpu.VMEM((256, 1024), F32),
            pltpu.VMEM((128, 256), F32),
            pltpu.VMEM((1, 256), F32),
            dma((6,)),
        ],
        compiler_params=pltpu.CompilerParams(vmem_limit_bytes=16 * 1024 * 1024),
    )(*handed)


def solution(mesh):
    placed = (
        P(None, "dp", None),
        P(None, "dp", None),
        P(None, "dp"),
        P(),
        P("section", None),
        P("section", None, None),
        P("section", None, None),
    )
    return jax.shard_map(
        shards,
        mesh=mesh,
        in_specs=placed,
        out_specs=(P("section", "dp", None), P("section", "dp", None), P("section", "dp")),
        check_vma=False,
    )
```

```python
import jax
import jax.numpy as jnp
from jax import lax
from jax.experimental import pallas as pl
from jax.experimental.pallas import tpu as pltpu
from jax.sharding import PartitionSpec as P

EPS = 1e-05
MESH = pl.DeviceIdType.MESH
F32 = jnp.float32
BF16 = jnp.bfloat16
VMEM_LIMIT = 44 * 1024 * 1024


def mm(a, b, dims=((1,), (0,))):
    return lax.dot_general(a, b, (dims, ((), ())), preferred_element_type=F32)


def mixing_pair(seg_row):
    rows = seg_row.shape[1]
    across = jnp.broadcast_to(seg_row, (rows, rows))
    down = across.T
    i = lax.broadcasted_iota(jnp.int32, (rows, rows), 0)
    j = lax.broadcasted_iota(jnp.int32, (rows, rows), 1)
    same = across == down
    low = jnp.where(same & (j <= i), 1.0, 0.0).astype(F32)
    high = jnp.where(same & (i <= j), 1.0, 0.0).astype(F32)
    mixing = (low / jnp.sum(low, axis=1, keepdims=True)).astype(BF16)
    mixing_t = (high / jnp.sum(high, axis=0, keepdims=True)).astype(BF16)
    return mixing, mixing_t


class Place:
    def __init__(self):
        self.s = lax.axis_index("section")
        self.d = lax.axis_index("dp")
        self.z = lax.div(self.s, 2)
        self.xl = lax.rem(self.s, 2)
        self.y = lax.div(self.d, 4)
        self.xh = lax.rem(lax.div(self.d, 2), 2)
        self.core = lax.rem(self.d, 2)
        x = self.xh * 2 + self.xl
        self.ys = [lax.rem(self.y + k, 4) for k in range(4)]
        self.xhs = [self.xh] + [lax.div(lax.rem(x + k, 4), 2) for k in range(1, 4)]
        self.twin = self.s + 1 - 2 * self.xl
        self.rows = [y * 4 for y in self.ys]

    def z_peer(self, k):
        return (lax.rem(self.z + k, 8) * 2 + self.xl, self.d)

    def member(self, dx, dy, core):
        section = self.s if dx % 2 == 0 else self.twin
        return (section, self.rows[dy] + self.xhs[dx] * 2 + core)

    def y_peer(self, k):
        return self.member(0, k, self.core)

    def x_peer(self, k):
        return self.member(k, 0, self.core)

    def core_peer(self):
        return self.member(0, 0, 1 - self.core)


def remote(src, dst, send_sem, recv_sem, peer):
    return pltpu.make_async_remote_copy(
        src_ref=src, dst_ref=dst, send_sem=send_sem, recv_sem=recv_sem,
        device_id=peer, device_id_type=MESH,
    )


def send(src, dst, send_sem, recv_sem, peer):
    copy = remote(src, dst, send_sem, recv_sem, peer)
    copy.start()
    return copy


def relay(
    basis_hbm, gain_hbm, value_hbm, out_hbm, c_hbm, cot_hbm, seg_hbm,
    whole, out, basis_own, value_own, folded_ref, own_gain_ref,
    value, value_cols, basis_half, basis, gain_half, gain, c_ref, cot_ref, seg_ref,
    part_n, part_nb, slot_n, gain_pad, every, xs, grads, es, hs, invs, left_t, part, part_b, slots, summed,
    load_sem, n_send, n_recv, z_send, z_recv, y_send, y_recv, x_send, x_recv, c_send, c_recv,
    rs_send, rs_recv, ag_send, ag_recv,
):
    at = Place()
    width = basis.shape[0]
    half = width // 2
    cuts = (0, 256, 768, 1280, 1792, 2048)
    start = pl.multiple_of(at.core * half, half)

    def load(i, src, dst):
        copy = pltpu.make_async_copy(src, dst, load_sem.at[i])
        copy.start()
        return copy

    gain_half_load = load(0, gain_hbm.at[:, pl.ds(start, half)], gain_half)
    early = []
    for i in range(len(cuts) - 1):
        size = cuts[i + 1] - cuts[i]
        rows, here = pl.ds(pl.multiple_of(start + cuts[i], 256), size), pl.ds(cuts[i], size)
        early.append((
            load(1 + 2 * i, basis_hbm.at[rows, :], basis_half.at[here, :]),
            load(2 + 2 * i, value_hbm.at[0, rows, :], value.at[here, :]),
        ))
    out_load = load(11, out_hbm.at[0], out)
    barrier = pltpu.get_barrier_semaphore()
    peers = [at.z_peer(k) for k in (4, 3, 5, 2, 6, 1, 7)]
    peers += [at.member(dx, dy, core) for dx in (1, 3) for dy in (2, 1, 3, 0) for core in (0, 1)]
    peers += [at.member(0, dy, core) for dy in (2, 1, 3) for core in (0, 1)] + [at.core_peer()]
    for peer in peers:
        pl.semaphore_signal(barrier, inc=1, device_id=peer, device_id_type=MESH)
    own_rows = pl.ds(pl.multiple_of(at.d * 256, 256), 256)
    cols = pl.ds(pl.multiple_of(lax.div(at.d, 2) * 128, 128), 128)

    gain_half_load.wait()
    wide = jnp.zeros((256, out.shape[0]), F32)
    for i in range(len(cuts) - 1):
        lanes = slice(cuts[i], cuts[i + 1])
        early[i][0].wait()
        scaled = (basis_half[lanes, :].astype(F32).T * gain_half[0:1, lanes]).astype(BF16)
        early[i][1].wait()
        if i == len(cuts) - 2:
            late = [
                load(12, basis_hbm, basis),
                load(13, value_hbm.at[0, :, cols], value_cols),
                load(14, gain_hbm, gain),
                load(15, c_hbm, c_ref),
                load(16, seg_hbm, seg_ref),
                load(17, cot_hbm, cot_ref),
                load(18, basis_hbm.at[own_rows, :], basis_own),
                load(19, value_hbm.at[0, own_rows, :], value_own),
            ]
        wide = wide + mm(scaled, value[lanes, :])
    out_load.wait()
    partial = mm(wide.astype(BF16), out[...])
    part_n[...] = partial.reshape(8, 32, 256)
    part_nb[...] = partial.astype(BF16).reshape(8, 32, 256)

    pl.semaphore_wait(barrier, len(peers))
    other = 1 - at.core
    swap = send(part_nb.at[other * 4 + at.y], slot_n, n_send, n_recv, at.core_peer())
    swap.wait_recv()
    own = every.at[at.core, at.z, at.xl, at.y]
    own[...] = (part_n[at.core * 4 + at.y] + slot_n[...].astype(F32)).astype(BF16)
    over_z = [send(own, own, z_send.at[k], z_recv.at[at.z], at.z_peer(k)) for k in (4, 3, 5, 2, 6, 1, 7)]

    for copy in late:
        copy.wait()
    gram = jnp.zeros((256, 256), F32)
    folded = jnp.zeros((256, 128), F32)
    for i in range(8):
        lanes = slice(i * 512, (i + 1) * 512)
        chunk = basis[lanes, :]
        chunk_t = chunk.astype(F32).T
        gram = gram + mm(chunk_t.astype(BF16), chunk)
        scaled = (chunk_t * gain[0:1, lanes]).astype(BF16)
        folded = folded + mm(scaled, value_cols[lanes, :])
    folded_ref[...] = folded.astype(BF16)
    gram_b = gram.astype(BF16)
    for i in range(16):
        gain_pad[i : i + 1, :] = gain[0:1, i * 256 : (i + 1) * 256]
    gain_pad[16:128, :] = jnp.zeros((112, 256), F32)
    gain_cols = gain_pad[...].T
    lane = lax.broadcasted_iota(jnp.int32, gain_cols.shape, 1)
    own_gain = jnp.sum(jnp.where(lane == at.d, gain_cols, 0.0), axis=1, keepdims=True)
    own_gain_ref[...] = jnp.broadcast_to(own_gain, own_gain_ref.shape)
    micros = c_ref.shape[0]
    mixings = [mixing_pair(seg_ref[m : m + 1, :].astype(F32)) for m in range(micros)]
    cs = [c_ref[m].astype(F32) for m in range(micros)]
    hh = [mm(c_ref[m], gram_b) for m in range(micros)]

    bounds = (0, 2, 4, 6, 8)
    over_y, over_x, across = [], [], []

    def arrived(z):
        @pl.when(at.z != z)
        def _():
            there = every.at[at.core, z, at.xl, at.y]
            remote(there, there, z_send.at[0], z_recv.at[z], at.core_peer()).wait_recv()

    def planes(q):
        return pl.ds(bounds[q], bounds[q + 1] - bounds[q])

    def start_y(q):
        for z in range(bounds[q], bounds[q + 1]):
            arrived(z)
        mine = every.at[at.core, planes(q), at.xl, at.y]
        over_y.append(
            [send(mine, mine, y_send.at[q, k], y_recv.at[q, k], at.y_peer(k)) for k in (2, 1, 3)]
        )

    def start_x(q):
        for copy in over_y[q]:
            copy.wait_recv()
        low = every.at[at.core, planes(q), at.xl, pl.ds(0, 2)]
        high = every.at[at.core, planes(q), at.xl, pl.ds(2, 2)]
        over_x.append([
            send(low, low, x_send.at[q, 0], x_recv.at[q, 0], at.x_peer(1)),
            send(high, high, x_send.at[q, 1], x_recv.at[q, 1], at.x_peer(3)),
        ])

    def start_core(q):
        for copy in over_x[q]:
            copy.wait_recv()
        chunk = every.at[at.core, planes(q)]
        across.append(send(chunk, chunk, c_send.at[q], c_recv.at[q], at.core_peer()))

    def sent(copies):
        for copy in copies:
            copy.wait_send()

    def step_of(s):
        z, xl = s // 2, s % 2
        return every[:, z, xl].reshape(256, 256)

    def onward(s):
        return mm(step_of(s), gram_b).astype(BF16)

    def forward(s, ng):
        n = step_of(s)
        both = range(micros)
        es_ = [mm(cs[m].astype(BF16), n) for m in both]
        invs_ = []
        for m in both:
            ms = jnp.sum(cs[m] * hh[m], axis=1, keepdims=True) * (1.0 / width)
            invs_.append(lax.rsqrt(jnp.maximum(ms, 0.0) + EPS))
        fs_ = [mm(cs[m].astype(BF16), ng) for m in both] if s < 15 else []
        old = list(cs)
        for m in both:
            xs[s, m] = (invs_[m] * old[m]).astype(BF16)
            es[s, m] = es_[m]
            hs[s, m] = hh[m]
            invs[s, m] = jnp.broadcast_to(invs_[m], invs.shape[2:])
        if s == 15:
            return None
        ys_ = [mm(mixings[m][0], (invs_[m] * es_[m]).astype(BF16)) for m in both]
        for m in both:
            cs[m] = cs[m] + ys_[m]
        ng = onward(s + 1)
        zs_ = [mm(mixings[m][0], (invs_[m] * fs_[m]).astype(BF16)) for m in both]
        for m in both:
            hh[m] = hh[m] + zs_[m]
        return ng

    start_y(0)
    start_y(1)
    sent(over_y[0])
    start_y(2)
    start_x(0)
    sent(over_y[1])
    start_y(3)
    start_x(1)
    start_core(0)
    start_x(2)
    start_core(1)
    start_x(3)
    across[0].wait_recv()
    ng = onward(0)
    for s in (0, 1, 2):
        ng = forward(s, ng)
    across[1].wait_recv()
    start_core(2)
    for s in (3, 4, 5, 6):
        ng = forward(s, ng)
    start_core(3)
    across[2].wait_recv()
    for s in (7, 8, 9, 10):
        ng = forward(s, ng)
    across[3].wait_recv()
    for s in (11, 12, 13, 14, 15):
        ng = forward(s, ng)

    twin = at.twin
    lanes_here = pl.ds(pl.multiple_of(at.xh * 128, 128), 128)
    lanes_over = pl.ds(pl.multiple_of((1 - at.xh) * 128, 128), 128)

    def left_factor(i, s, lanes):
        for m in range(micros):
            mixed = mm(mixings[m][0], xs[s, m, :, lanes])
            left_t[i, :, m * 128 : (m + 1) * 128] = mixed.T.astype(BF16)

    gs = [cot_ref[m].astype(F32) for m in range(micros)]
    both = range(micros)
    for s in reversed(range(16)):
        for m in both:
            grads[s, m] = gs[m].astype(BF16)
        if s == 0:
            break
        n = step_of(s)
        ps_ = [mm(mixings[m][1], gs[m].astype(BF16)) for m in both]
        qs_ = [mm(p.astype(BF16), n, ((1,), (1,))) for p in ps_]
        for m in both:
            inv = invs[s, m][:, :1]
            t = jnp.sum(ps_[m] * es[s, m], axis=1, keepdims=True)
            gs[m] = (gs[m] - (inv * inv * inv * t * (1.0 / width)) * hs[s, m]) + inv * qs_[m]
        if s == 15:
            left_factor(0, twin, lanes_here)
        if s == 14:
            left_factor(1, at.s, lanes_over)

    rows = micros * 128
    over = mm(left_t[1], grads[at.s].reshape(rows, 256))
    part_b[1] = over.astype(BF16).reshape(4, 32, 256)
    pieces = []
    for i, dy in enumerate((2, 1, 3, 0)):
        j = 2 * i + at.core
        pieces.append(send(
            part_b.at[1, at.ys[dy]], slots.at[j], rs_send.at[i], rs_recv.at[j],
            (at.twin, at.rows[dy] + (1 - at.xh) * 2 + 1)))
    here = mm(left_t[0], grads[twin].reshape(rows, 256))
    part[...] = here.reshape(4, 32, 256)
    part_b[0] = here.astype(BF16).reshape(4, 32, 256)
    for i, dy in enumerate((2, 1, 3)):
        j = 8 + 2 * i + at.core
        pieces.append(send(
            part_b.at[0, at.ys[dy]], slots.at[j], rs_send.at[4 + i], rs_recv.at[j],
            at.member(0, dy, 1)))
    beside = remote(part_b.at[0, at.y], slots.at[14], rs_send.at[7], rs_recv.at[14], at.core_peer())
    place = whole.at[at.xh, at.y]
    spread = [
        remote(summed, place, ag_send.at[i, j], ag_recv.at[i, j], at.member(dx, dy, at.core))
        for i, dy in enumerate((2, 1, 3, 0)) for j, dx in enumerate((1, 3))
    ]
    hand = remote(summed, summed, rs_send.at[8], rs_recv.at[15], at.core_peer())

    @pl.when(at.core == 0)
    def _():
        beside.start()
        hand.wait_recv()

    @pl.when(at.core == 1)
    def _():
        mine = part[at.y]
        for j in (14, 12, 13, 10, 11, 8, 9, 6, 7, 4, 5, 2, 3, 0, 1):
            remote(slots.at[j], slots.at[j], rs_send.at[0], rs_recv.at[j], at.core_peer()).wait_recv()
            mine = mine + slots[j].astype(F32)
        summed[...] = mine.astype(BF16)
        hand.start()

    for copy in spread:
        copy.start()
    sent([swap] + over_z + sum(over_y[2:], []) + sum(over_x, []) + across + pieces)
    sent(spread)

    @pl.when(at.core == 0)
    def _():
        beside.wait_send()

    @pl.when(at.core == 1)
    def _():
        hand.wait_send()

    for i, dy in enumerate((2, 1, 3, 0)):
        for j, dx in enumerate((1, 3)):
            there = whole.at[at.xhs[4 - dx], at.ys[(4 - dy) % 4]]
            remote(there, there, ag_send.at[0, 0], ag_recv.at[i, j], at.core_peer()).wait_recv()


def finish(factor_ref, out, basis, value, folded, own_gain, gv_hbm, go_hbm, gg_hbm,
           gv, go, gg, store_sem):
    d = lax.axis_index("dp")
    factor = factor_ref[...].reshape(256, 256)
    left = mm(basis[...], factor).astype(BF16)
    gain = own_gain[:, :1]
    sums = jnp.zeros((256, 1), F32)
    stores = []
    for i in range(4):
        lanes = slice(i * 256, (i + 1) * 256)
        plain = mm(left, out[lanes, :], ((1,), (1,)))
        gv[:, lanes] = gain * plain
        stores.append(pltpu.make_async_copy(
            gv.at[:, lanes], gv_hbm.at[0, :, lanes], store_sem.at[i]))
        stores[-1].start()
        sums = sums + jnp.sum(plain * value[:, lanes].astype(F32), axis=1, keepdims=True)
    go[...] = mm(folded[...], factor, ((0,), (0,)))
    own = pl.ds(pl.multiple_of((d % 2) * 64, 64), 64)
    stores.append(pltpu.make_async_copy(go.at[own, :], go_hbm.at[0], store_sem.at[4]))
    stores[-1].start()
    gg[...] = jnp.broadcast_to(sums, (256, 128)).T[0:1, :]
    stores.append(pltpu.make_async_copy(gg, gg_hbm, store_sem.at[5]))
    stores[-1].start()
    for store in stores:
        store.wait()


def shards(coeffs, cotangent, segment_ids, basis_matrix, section_gains, value_weight, out_weight):
    vmem = pl.BlockSpec(memory_space=pltpu.VMEM)
    hbm = pl.BlockSpec(memory_space=pltpu.HBM)
    dma = pltpu.SemaphoreType.DMA
    shape = jax.ShapeDtypeStruct
    operands = (basis_matrix, section_gains, value_weight, out_weight, coeffs, cotangent, segment_ids)
    operands = [pltpu.with_memory_space_constraint(x, pltpu.HBM) for x in operands]
    handed = pl.pallas_call(
        relay,
        out_shape=(
            shape((2, 4, 32, 256), BF16),
            shape((1024, 256), BF16),
            shape((256, 256), BF16),
            shape((256, 1024), BF16),
            shape((256, 128), BF16),
            shape((256, 128), F32),
        ),
        in_specs=[hbm] * 7,
        out_specs=(vmem,) * 6,
        scratch_shapes=[
            pltpu.VMEM((2048, 1024), BF16),
            pltpu.VMEM((4096, 128), BF16),
            pltpu.VMEM((2048, 256), BF16),
            pltpu.VMEM((4096, 256), BF16),
            pltpu.VMEM((1, 2048), F32),
            pltpu.VMEM((1, 4096), F32),
            pltpu.VMEM((2, 128, 256), BF16),
            pltpu.VMEM((2, 128, 256), BF16),
            pltpu.VMEM((2, 128), jnp.int32),
            pltpu.VMEM((8, 32, 256), F32),
            pltpu.VMEM((8, 32, 256), BF16),
            pltpu.VMEM((32, 256), BF16),
            pltpu.VMEM((128, 256), F32),
            pltpu.VMEM((2, 8, 2, 4, 32, 256), BF16),
            pltpu.VMEM((16, 2, 128, 256), BF16),
            pltpu.VMEM((16, 2, 128, 256), BF16),
            pltpu.VMEM((16, 2, 128, 256), F32),
            pltpu.VMEM((16, 2, 128, 256), F32),
            pltpu.VMEM((16, 2, 128, 128), F32),
            pltpu.VMEM((2, 128, 256), BF16),
            pltpu.VMEM((4, 32, 256), F32),
            pltpu.VMEM((2, 4, 32, 256), BF16),
            pltpu.VMEM((15, 32, 256), BF16),
            pltpu.VMEM((32, 256), BF16),
            dma((20,)), dma, dma, dma((8,)), dma((8,)),
            dma((4, 4)), dma((4, 4)), dma((4, 2)), dma((4, 2)), dma((4,)), dma((4,)),
            dma((9,)), dma((16,)), dma((4, 2)), dma((4, 2)),
        ],
        compiler_params=pltpu.CompilerParams(
            collective_id=0, has_side_effects=True, vmem_limit_bytes=VMEM_LIMIT
        ),
    )(*operands)
    return pl.pallas_call(
        finish,
        out_shape=(
            shape((1, 256, 1024), F32),
            shape((1, 64, 256), F32),
            shape((1, 256), F32),
        ),
        in_specs=[vmem] * 6,
        out_specs=(hbm,) * 3,
        scratch_shapes=[
            pltpu.VMEM((256, 1024), F32),
            pltpu.VMEM((128, 256), F32),
            pltpu.VMEM((1, 256), F32),
            dma((6,)),
        ],
        compiler_params=pltpu.CompilerParams(vmem_limit_bytes=16 * 1024 * 1024),
    )(*handed)


def solution(mesh):
    placed = (
        P(None, "dp", None),
        P(None, "dp", None),
        P(None, "dp"),
        P(),
        P("section", None),
        P("section", None, None),
        P("section", None, None),
    )
    return jax.shard_map(
        shards,
        mesh=mesh,
        in_specs=placed,
        out_specs=(P("section", "dp", None), P("section", "dp", None), P("section", "dp")),
        check_vma=False,
    )
```
